32 devices in a mesh: dp: 4 (over z), ctx: 8 (over y, x, core).
Axes of the slice: x: 2, y: 2, z: 4, core: 2. Of those that a mesh axis runs over, the one named last changes fastest.
Arguments:
- queries: bfloat16 [8192, 4096], P(('dp', 'ctx')), parts along dimension 0, may hold values from -5 to 5
- keys_values: bfloat16 [8192, 2, 1024], P(('dp', 'ctx')), parts along dimension 0, may hold values from -5 to 5
- fold: int32 [64], P('dp'), parts along dimension 0, may hold values from 0 to 15, each once
- doc_length: int32 [4], P('dp'), parts along dimension 0, may hold values from 1024 to 2048
Outputs:
- attended: bfloat16 [8192, 4096], P(('dp', 'ctx')), parts along dimension 0
The draws below stay inside these ranges and needn't reach their ends.
There are 4 independent parts, one for each index of `dp`. The reference program is written for one: setup_inputs(seed, part) draws one part's arguments, and reference() takes and returns one part's arrays. A program takes and returns all parts, laid end to end along the dimension named above; each array names one. Nothing has to cross between parts.
Inputs may be any that keep to these rules, and one draw needn't show every extreme that they name: A permutation: slot s, the stored rows s * 128 to (s + 1) * 128 - 1, holds positions fold[s] * 128 onwards. `doc_length`: positions at or beyond it are padding.
All inputs are finite; a program needn't handle non-finite values.
Results may differ from the reference program's by a relative error of at most 0.004.
Values may be sent and summed in bfloat16 or wider, within the bound.
No kernel may reach another device: no remote copies, remote signals or barrier semaphores. Data moves between devices by JAX's collectives and lax.ppermute only.
A program may use at most 320 MiB of HBM per device.

```python
import math
import jax
import jax.numpy as jnp
from jax import lax

HEADS = 32
KV_HEADS = 8
HEAD_DIM = 128
SPAN = 128
SPANS = 16
TOKENS = 2048


def draw_queries(key, part):
    width = HEADS * HEAD_DIM
    result = jnp.clip(1.5 * jax.random.normal(jax.random.fold_in(key, 1), (TOKENS, width), jnp.float32), -5.0, 5.0)
    return result.astype(jnp.bfloat16)


def draw_keys_values(key, part):
    width = KV_HEADS * HEAD_DIM
    key_part = jnp.clip(1.5 * jax.random.normal(jax.random.fold_in(key, 2), (TOKENS, width), jnp.float32), -5.0, 5.0)
    value_part = jnp.clip(jax.random.normal(jax.random.fold_in(key, 3), (TOKENS, width), jnp.float32), -5.0, 5.0)
    return jnp.stack([key_part, value_part], axis=1).astype(jnp.bfloat16)


def setup_inputs(seed: int = 0, part: int = 0) -> dict:
    seeds = jax.random.split(jax.random.key(seed), 5)
    part_keys = jax.random.split(jax.random.fold_in(seeds[4], part), 5)
    queries = draw_queries(jax.random.fold_in(jax.random.fold_in(seeds[4], part), 71), part)
    keys_values = draw_keys_values(jax.random.fold_in(jax.random.fold_in(seeds[4], part), 71), part)
    fold = jax.random.permutation(part_keys[2], SPANS).astype(jnp.int32)
    doc_length = jax.random.randint(part_keys[3], (1,), TOKENS // 2, TOKENS + 1).astype(jnp.int32)
    return {"queries": queries, "keys_values": keys_values, "fold": fold, "doc_length": doc_length}


def positions(fold, row_count, span_rows):
    row_ids = jnp.arange(row_count, dtype=jnp.int32)
    slot_ids = (row_ids // span_rows).astype(jnp.int32)
    return fold[slot_ids] * span_rows + row_ids % span_rows

def reference(queries, keys_values, fold, doc_length):
    position = positions(fold, TOKENS, SPAN)
    length = doc_length[0]
    visible = (position[None, :] <= position[:, None]) & (position[None, :] < length)
    group_size = HEADS // KV_HEADS
    score_scale = 1.0 / math.sqrt(HEAD_DIM)
    query_heads = queries.reshape(TOKENS, KV_HEADS, group_size, HEAD_DIM).transpose(1, 2, 0, 3)
    key_heads = keys_values[:, 0].reshape(TOKENS, KV_HEADS, HEAD_DIM).transpose(1, 0, 2)
    value_heads = keys_values[:, 1].reshape(TOKENS, KV_HEADS, HEAD_DIM).transpose(1, 0, 2)

    def one_group(operands):
        query_group, key_block, value_block = operands

        def one_head(query_head):
            scores = jnp.dot(query_head, key_block.T, preferred_element_type=jnp.float32) * score_scale
            scores = jnp.where(visible, scores, -1e+30)
            row_max = lax.optimization_barrier(jnp.max(scores, axis=1, keepdims=True))
            weights = jnp.where(visible, jnp.exp(scores - row_max), 0.0)
            weight_sum = lax.optimization_barrier(jnp.sum(weights, axis=1, keepdims=True))
            numerator = jnp.dot(weights.astype(jnp.bfloat16), value_block, preferred_element_type=jnp.float32)
            return numerator / weight_sum
        return lax.map(one_head, query_group)
    result = lax.map(one_group, (query_heads, key_heads, value_heads))
    result = result.transpose(2, 0, 1, 3).reshape(TOKENS, HEADS * HEAD_DIM)
    result = jnp.where((position < length)[:, None], result, 0.0)
    return result.astype(jnp.bfloat16)
```

```python
import functools
import math

import jax
import jax.numpy as jnp
from jax import lax
from jax.experimental import pallas as pl
from jax.experimental.pallas import tpu as pltpu
from jax.sharding import PartitionSpec as P

HEADS = 32
KV_HEADS = 8
HEAD_DIM = 128
GROUP = HEADS // KV_HEADS
CHUNKS = (2, 2, 2, 2)
KEY_SPANS = 4
SCALE = math.log2(math.e) / math.sqrt(HEAD_DIM)
LOW, HIGH = 2.0**-90, 2.0**90


def attend(offsets, heads, first_head, spans, span_rows, table, q_ref, *refs):
    count = len(offsets)
    sources = refs[:count]
    out_ref, key_buf, value_buf, total, result, flag, sem = refs[-7:]
    me = table[spans + 1]
    length = table[spans]
    group_rows = GROUP * span_rows
    block = KEY_SPANS * span_rows

    ones = jnp.ones((span_rows, HEAD_DIM), jnp.bfloat16)
    for (offset, first), source in zip(offsets, sources):
        for j in range(source.shape[1] // span_rows):
            place = table[2 * (me ^ offset) + first + j]
            rows = slice(j * span_rows, (j + 1) * span_rows)
            at = pl.ds(pl.multiple_of(place * span_rows, span_rows), span_rows)
            for g in range(heads):
                cols = slice(g * HEAD_DIM, (g + 1) * HEAD_DIM)
                key_buf[g, at, :] = source[0, rows, cols]
                value_buf[g, at, :HEAD_DIM] = source[1, rows, cols]
                value_buf[g, at, HEAD_DIM:] = ones

    def query_of(i, g):
        rows = slice(i * span_rows, (i + 1) * span_rows)
        return jnp.concatenate(
            [
                q_ref[rows, ((first_head + g) * GROUP + n) * HEAD_DIM : ((first_head + g) * GROUP + n + 1) * HEAD_DIM]
                for n in range(GROUP)
            ],
            axis=0,
        )

    def scores_of(i, g, at):
        return SCALE * lax.dot_general(
            query_of(i, g), key_buf[g, at, :], (((1,), (1,)), ((), ())), preferred_element_type=jnp.float32
        )

    def limits(place):
        row = lax.broadcasted_iota(jnp.int32, (group_rows, 1), 0) % span_rows
        return jnp.minimum(place * span_rows + row, length - 1)

    def seen(place, k):
        key_pos = k * block + lax.broadcasted_iota(jnp.int32, (group_rows, block), 1)
        return key_pos <= limits(place)

    def key_rows(k):
        return pl.ds(pl.multiple_of(k * block, block), block)

    def finish(i, g, place):
        row = place * span_rows + lax.broadcasted_iota(jnp.int32, (group_rows, 1), 0) % span_rows
        weight_sum = total[i, g, :, HEAD_DIM:]
        value = jnp.where(row < length, total[i, g, :, :HEAD_DIM] / weight_sum, 0.0).astype(jnp.bfloat16)
        for n in range(GROUP):
            c = (g * GROUP + n) * HEAD_DIM
            result[i * span_rows : (i + 1) * span_rows, c : c + HEAD_DIM] = value[n * span_rows : (n + 1) * span_rows]
        fine = (weight_sum > LOW) & (weight_sum < HIGH) | (row >= length)
        flag[...] = jnp.where(fine, flag[...], 1.0)

    flag[...] = jnp.zeros_like(flag)
    for i in range(2):
        place = table[2 * me + i]
        real = place * span_rows < length

        @pl.when(real)
        def _():
            def whole(k, carry):
                at = key_rows(k)
                for g in range(heads):
                    weights = jnp.exp2(scores_of(i, g, at)).astype(jnp.bfloat16)
                    total[i, g] += jnp.dot(weights, value_buf[g, at, :], preferred_element_type=jnp.float32)
                return carry

            last = place // KEY_SPANS
            at = key_rows(last)
            mask = seen(place, last)
            for g in range(heads):
                weights = jnp.where(mask, jnp.exp2(scores_of(i, g, at)), 0.0).astype(jnp.bfloat16)
                total[i, g] = jnp.dot(weights, value_buf[g, at, :], preferred_element_type=jnp.float32)
            lax.fori_loop(0, last, whole, 0)
            for g in range(heads):
                finish(i, g, place)

        @pl.when(jnp.logical_not(real))
        def _():
            result[i * span_rows : (i + 1) * span_rows, :] = jnp.zeros(
                (span_rows, heads * GROUP * HEAD_DIM), jnp.bfloat16
            )

    @pl.when(jnp.max(flag[...]) > 0.0)
    def _():
        for i in range(2):
            place = table[2 * me + i]

            @pl.when(place * span_rows < length)
            def _():
                def one_head(g, carry):
                    q0 = pl.multiple_of((first_head + g) * GROUP * HEAD_DIM, GROUP * HEAD_DIM)
                    rows = slice(i * span_rows, (i + 1) * span_rows)

                    def masked(n, k):
                        query = q_ref[rows, pl.ds(pl.multiple_of(q0 + n * HEAD_DIM, HEAD_DIM), HEAD_DIM)]
                        raw = SCALE * lax.dot_general(
                            query, key_buf[g, key_rows(k), :], (((1,), (1,)), ((), ())),
                            preferred_element_type=jnp.float32,
                        )
                        key_pos = k * block + lax.broadcasted_iota(jnp.int32, (span_rows, block), 1)
                        row = lax.broadcasted_iota(jnp.int32, (span_rows, 1), 0)
                        mask = key_pos <= jnp.minimum(place * span_rows + row, length - 1)
                        return raw, mask

                    def one(n, carry):
                        def top(k, peak):
                            raw, mask = masked(n, k)
                            return jnp.maximum(peak, jnp.max(jnp.where(mask, raw, -1e30), axis=1, keepdims=True))

                        blocks = place // KEY_SPANS + 1
                        peak = lax.fori_loop(0, blocks, top, jnp.full((span_rows, 1), -1e30, jnp.float32))

                        def add(k, acc):
                            raw, mask = masked(n, k)
                            weights = jnp.where(mask, jnp.exp2(raw - peak), 0.0).astype(jnp.bfloat16)
                            return acc + jnp.dot(
                                weights, value_buf[g, key_rows(k), :], preferred_element_type=jnp.float32
                            )

                        acc = lax.fori_loop(0, blocks, add, jnp.zeros((span_rows, 2 * HEAD_DIM), jnp.float32))
                        row = place * span_rows + lax.broadcasted_iota(jnp.int32, (span_rows, 1), 0)
                        value = jnp.where(row < length, acc[:, :HEAD_DIM] / acc[:, HEAD_DIM:], 0.0)
                        c = pl.multiple_of((g * GROUP + n) * HEAD_DIM, HEAD_DIM)
                        result[rows, pl.ds(c, HEAD_DIM)] = value.astype(jnp.bfloat16)
                        return carry

                    return lax.fori_loop(0, GROUP, one, carry)

                lax.fori_loop(0, heads, one_head, 0)

    width = heads * GROUP * HEAD_DIM
    start = first_head * GROUP * HEAD_DIM
    copy = pltpu.make_async_copy(result, out_ref.at[:, start : start + width], sem)
    copy.start()
    copy.wait()


def attention_chunk(table, queries, sources, offsets, attended, heads, first_head, spans):
    rows = queries.shape[0]
    span_rows = rows // 2
    width = heads * GROUP * HEAD_DIM
    vmem = pl.BlockSpec(memory_space=pltpu.VMEM)
    kernel = functools.partial(attend, offsets, heads, first_head, spans, span_rows)
    keys = spans * span_rows
    before = [] if attended is None else [attended]
    return pl.pallas_call(
        kernel,
        out_shape=jax.ShapeDtypeStruct(queries.shape, jnp.bfloat16),
        in_specs=[pl.BlockSpec(memory_space=pltpu.SMEM), vmem]
        + [vmem] * len(sources)
        + [pl.BlockSpec(memory_space=pl.ANY)] * len(before),
        out_specs=pl.BlockSpec(memory_space=pl.ANY),
        scratch_shapes=[
            pltpu.VMEM((heads, keys, HEAD_DIM), jnp.bfloat16),
            pltpu.VMEM((heads, keys, 2 * HEAD_DIM), jnp.bfloat16),
            pltpu.VMEM((2, heads, GROUP * span_rows, 2 * HEAD_DIM), jnp.float32),
            pltpu.VMEM((rows, width), jnp.bfloat16),
            pltpu.VMEM((GROUP * span_rows, HEAD_DIM), jnp.float32),
            pltpu.SemaphoreType.DMA,
        ],
        input_output_aliases={2 + len(sources): 0} if before else {},
        compiler_params=pltpu.CompilerParams(vmem_limit_bytes=40 << 20),
        cost_estimate=pl.CostEstimate(
            flops=rows * heads * GROUP * keys * HEAD_DIM * 4, bytes_accessed=4 * keys * heads * HEAD_DIM, transcendentals=0
        ),
        name="attend",
    )(table, queries, *sources, *before)


def shards(queries, keys_values, fold, doc_length):
    size = lax.axis_size("ctx")
    me = lax.axis_index("ctx")
    rows = queries.shape[0]
    half = rows // 2
    spans = fold.shape[0]
    table = jnp.concatenate([fold, doc_length, me[None].astype(jnp.int32)])

    def swap(block, mask):
        return lax.ppermute(block, "ctx", [(i, i ^ mask) for i in range(size)])

    chip_offsets = sorted(range(0, size, 2), key=lambda o: (bin(o).count("1"), o))
    split = jnp.transpose(keys_values, (1, 0, 2))
    attended = None
    first_head = 0
    for heads in CHUNKS:
        cols = slice(first_head * HEAD_DIM, (first_head + heads) * HEAD_DIM)
        held = {}
        for offset in chip_offsets:
            bits = [1 << b for b in range(1, size.bit_length()) if offset >> b & 1]
            if not bits:
                held[offset] = [(split[:, :, cols], 0)]
            elif len(bits) == 1:
                held[offset] = [(swap(held[0][0][0], offset), 0)]
            else:
                low, high = bits[0], bits[-1]

                def part(source, first):
                    if len(source) == 1:
                        return source[0][0][:, first * half : (first + 1) * half]
                    return source[first][0]

                held[offset] = [
                    (swap(part(held[offset ^ low], 0), low), 0),
                    (swap(part(held[offset ^ high], 1), high), 1),
                ]
        sources, offsets = [], []
        for offset in chip_offsets:
            for block, first in held[offset]:
                sources += [block, swap(block, 1)]
                offsets += [(offset, first), (offset ^ 1, first)]
        attended = attention_chunk(table, queries, sources, offsets, attended, heads, first_head, spans)
        first_head += heads
    return attended


def solution(mesh):
    in_specs = (P(("dp", "ctx"), None), P(("dp", "ctx"), None, None), P("dp"), P("dp"))
    out_specs = P(("dp", "ctx"), None)
    return jax.shard_map(shards, mesh=mesh, in_specs=in_specs, out_specs=out_specs, check_vma=False)
```

```python
import functools
import math

import jax
import jax.numpy as jnp
from jax import lax
from jax.experimental import pallas as pl
from jax.experimental.pallas import tpu as pltpu
from jax.sharding import PartitionSpec as P

HEADS = 32
KV_HEADS = 8
HEAD_DIM = 128
GROUP = HEADS // KV_HEADS
HEADS_AT_ONCE = 4
SCALE = math.log2(math.e) / math.sqrt(HEAD_DIM)
LOW, HIGH = 2.0**-90, 2.0**90
NT = (((1,), (1,)), ((), ()))


class Span:
    def __init__(self, pack, index, offset, core, later):
        self.pack, self.index, self.offset, self.core, self.later = pack, index, offset, core, later

    def place(self, table, spans):
        me = table[spans + 1]
        odd = me % 2
        offset = self.offset[0] + odd * (self.offset[1] - self.offset[0])
        core = self.core[0] + odd * (self.core[1] - self.core[0])
        device = ((me - odd) ^ offset) + core
        first, second = table[2 * device], table[2 * device + 1]
        return jnp.maximum(first, second) if self.later else jnp.minimum(first, second)


def stage(held, everything, n_packs, spans, is_first, is_last, *refs):
    refs = list(refs)
    table, q_ref = refs[:2]
    packs = refs[2 : 2 + n_packs]
    rest = refs[2 + n_packs :]
    if not is_first:
        before, rest = rest[0], rest[1:]
    if is_last:
        every = rest[: len({s.pack for s in everything})]
        rest = rest[len(every) :]
        out_hbm, key_buf, value_buf, out_ref, flag, keys_all, values_all, out_sems, sem = rest
        flag[...] = jnp.zeros_like(flag)
    else:
        total, key_buf, value_buf = rest
    span_rows = q_ref.shape[0] // 2
    group_rows = GROUP * span_rows
    me = table[spans + 1]
    length = table[spans]
    count = len(held)

    places = [s.place(table, spans) for s in held]
    for s, place in zip(held, places):
        rank = sum((other < place).astype(jnp.int32) for other in places)
        at = pl.ds(pl.multiple_of(rank * span_rows, span_rows), span_rows)
        key_buf[at, :] = packs[s.pack][s.index, 0]
        value_buf[at, :] = packs[s.pack][s.index, 1]

    def column(head):
        return pl.ds(pl.multiple_of(head * HEAD_DIM, HEAD_DIM), HEAD_DIM)

    def rows_of(i):
        return pl.ds(pl.multiple_of(i * span_rows, span_rows), span_rows)

    def row_in_span():
        return lax.broadcasted_iota(jnp.int32, (group_rows, 1), 0) % span_rows

    def finish(i, g, place, sums):
        real = place * span_rows + row_in_span() < length
        weight_sum = sums[:, HEAD_DIM:]
        value = jnp.where(real, sums[:, :HEAD_DIM] / weight_sum, 0.0).astype(jnp.bfloat16)
        for n in range(GROUP):
            out_ref[rows_of(i), column(g * GROUP + n)] = value[n * span_rows : (n + 1) * span_rows]
        fine = (weight_sum > LOW) & (weight_sum < HIGH) | jnp.logical_not(real)
        flag[...] = jnp.where(fine, flag[...], 1.0)

    def add(i, place, seen):
        if is_first:
            col = lax.broadcasted_iota(jnp.int32, (group_rows, span_rows), 1)
            mask = col <= jnp.minimum(row_in_span(), length - 1 - place * span_rows)

        def some_heads(step, carry):
            for h in range(HEADS_AT_ONCE):
                g = step * HEADS_AT_ONCE + h
                if seen:
                    query = jnp.concatenate([q_ref[rows_of(i), column(g * GROUP + n)] for n in range(GROUP)], axis=0)
                    scores = lax.dot_general(
                        query, key_buf[: seen * span_rows, column(g)], NT, preferred_element_type=jnp.float32
                    )
                    weights = jnp.exp2(scores * SCALE)
                    if is_first:
                        own = jnp.where(mask, weights[:, (seen - 1) * span_rows :], 0.0)
                        parts = [weights[:, : (seen - 1) * span_rows], own]
                        weights = jnp.concatenate(parts, axis=1) if seen > 1 else own
                    ones = jnp.ones((seen * span_rows, HEAD_DIM), jnp.bfloat16)
                    values = jnp.concatenate([value_buf[: seen * span_rows, column(g)], ones], axis=1)
                    product = jnp.dot(weights.astype(jnp.bfloat16), values, preferred_element_type=jnp.float32)
                if is_first:
                    total[i, g] = product
                elif not is_last:
                    total[i, g] = before[i, g] + product
                else:
                    finish(i, g, place, before[i, g] + product if seen else before[i, g])
            return carry

        lax.fori_loop(0, KV_HEADS // HEADS_AT_ONCE, some_heads, 0)

    def one_span(i, carry):
        place = table[2 * me + i]
        seen = sum((other <= place).astype(jnp.int32) for other in places)
        seen = jnp.where(place * span_rows < length, seen, 0)

        for n in range(0 if is_last else 1, count + 1):

            @pl.when(seen == n)
            def _():
                add(i, place, n)

        if is_last:
            pltpu.make_async_copy(out_ref.at[rows_of(i)], out_hbm.at[rows_of(i)], out_sems.at[i]).start()
        return carry

    lax.fori_loop(0, 2, one_span, 0)
    if not is_last:
        return

    for i in range(2):
        pltpu.make_async_copy(out_ref.at[rows_of(i)], out_hbm.at[rows_of(i)], out_sems.at[i]).wait()

    @pl.when(jnp.max(flag[...]) > 0.0)
    def _():
        block = 4 * span_rows

        def one_head(g, carry):
            for s in everything:
                at = pl.ds(pl.multiple_of(s.place(table, spans) * span_rows, span_rows), span_rows)
                for kind, target in enumerate((keys_all, values_all)):
                    copy = pltpu.make_async_copy(every[s.pack].at[s.index, kind, :, column(g)], target.at[at, :], sem)
                    copy.start()
                    copy.wait()

            def one(step, carry):
                i, n = step // GROUP, step % GROUP
                place = table[2 * me + i]
                rows = pl.ds(pl.multiple_of(i * span_rows, span_rows), span_rows)
                query = q_ref[rows, column(g * GROUP + n)]
                row = place * span_rows + lax.broadcasted_iota(jnp.int32, (span_rows, 1), 0)

                def masked(k):
                    at = pl.ds(pl.multiple_of(k * block, block), block)
                    raw = SCALE * lax.dot_general(query, keys_all[at, :], NT, preferred_element_type=jnp.float32)
                    key_pos = k * block + lax.broadcasted_iota(jnp.int32, (span_rows, block), 1)
                    return raw, key_pos <= jnp.minimum(row, length - 1), at

                def top(k, peak):
                    raw, mask, _ = masked(k)
                    return jnp.maximum(peak, jnp.max(jnp.where(mask, raw, -1e30), axis=1, keepdims=True))

                blocks = place // 4 + 1
                peak = lax.fori_loop(0, blocks, top, jnp.full((span_rows, 1), -1e30, jnp.float32))

                def more(k, sums):
                    raw, mask, at = masked(k)
                    weights = jnp.where(mask, jnp.exp2(raw - peak), 0.0)
                    product = jnp.dot(weights.astype(jnp.bfloat16), values_all[at, :], preferred_element_type=jnp.float32)
                    return sums[0] + product, sums[1] + jnp.sum(weights, axis=1, keepdims=True)

                zero = (jnp.zeros((span_rows, HEAD_DIM), jnp.float32), jnp.zeros((span_rows, 1), jnp.float32))
                numerator, weight_sum = lax.fori_loop(0, blocks, more, zero)
                value = jnp.where(row < length, numerator / weight_sum, 0.0)
                out_ref[rows, column(g * GROUP + n)] = value.astype(jnp.bfloat16)
                return carry

            return lax.fori_loop(0, 2 * GROUP, one, carry)

        lax.fori_loop(0, KV_HEADS, one_head, 0)
        copy = pltpu.make_async_copy(out_ref, out_hbm, sem)
        copy.start()
        copy.wait()


def run_stage(table, queries, packs, before, held, everything, spans, is_last, all_packs):
    rows = queries.shape[0]
    span_rows = rows // 2
    vmem = pl.BlockSpec(memory_space=pltpu.VMEM)
    hbm = pl.BlockSpec(memory_space=pl.ANY)
    names = sorted({s.pack for s in held})
    held = [Span(names.index(s.pack), s.index, s.offset, s.core, s.later) for s in held]
    operands = [table, queries] + [packs[n] for n in names]
    specs = [pl.BlockSpec(memory_space=pltpu.SMEM), vmem] + [vmem] * len(names)
    sums = (2, KV_HEADS, GROUP * span_rows, 2 * HEAD_DIM)
    keys = len(held) * span_rows
    scratch = [
        pltpu.VMEM((keys, KV_HEADS * HEAD_DIM), jnp.bfloat16),
        pltpu.VMEM((keys, KV_HEADS * HEAD_DIM), jnp.bfloat16),
    ]
    aliases = {}
    if before is not None:
        operands.append(before)
        specs.append(vmem)
    if is_last:
        operands += all_packs
        specs += [hbm] * len(all_packs)
        out_shape = jax.ShapeDtypeStruct(queries.shape, jnp.bfloat16)
        scratch += [
            pltpu.VMEM(queries.shape, jnp.bfloat16),
            pltpu.VMEM((GROUP * span_rows, HEAD_DIM), jnp.float32),
            pltpu.VMEM((spans * span_rows, HEAD_DIM), jnp.bfloat16),
            pltpu.VMEM((spans * span_rows, HEAD_DIM), jnp.bfloat16),
            pltpu.SemaphoreType.DMA((2,)),
            pltpu.SemaphoreType.DMA,
        ]
    else:
        out_shape = jax.ShapeDtypeStruct(sums, jnp.float32)
        if before is not None:
            aliases = {len(operands) - 1: 0}
    return pl.pallas_call(
        functools.partial(stage, held, everything, len(names), spans, before is None, is_last),
        out_shape=out_shape,
        in_specs=specs,
        out_specs=hbm if is_last else vmem,
        scratch_shapes=scratch,
        input_output_aliases=aliases,
        compiler_params=pltpu.CompilerParams(vmem_limit_bytes=24 << 20),
        cost_estimate=pl.CostEstimate(
            flops=rows * HEADS * keys * HEAD_DIM * 4, bytes_accessed=8 * keys * KV_HEADS * HEAD_DIM, transcendentals=0
        ),
        name="stage",
    )(*operands)


def shards(queries, keys_values, fold, doc_length):
    size = lax.axis_size("ctx")
    me = lax.axis_index("ctx")
    core = me % 2
    rows = queries.shape[0]
    spans = fold.shape[0]
    table = jnp.concatenate([fold, doc_length, me[None].astype(jnp.int32)])

    def swap(block, mask=1):
        return lax.ppermute(block, "ctx", [(i, i ^ mask) for i in range(size)])

    def both_links(block):
        return lax.ppermute(block, "ctx", [(i, i ^ (3 if i % 2 == 0 else 5)) for i in range(size)])

    halves = fold.reshape(size, 2)
    turned = jnp.sum(jnp.where(jnp.arange(size) == me, halves[:, 0] > halves[:, 1], False).astype(jnp.int32))
    half = rows // 2

    def span(start):
        return lax.dynamic_slice_in_dim(keys_values, start, half).transpose(1, 0, 2)[None]

    low, high = span(turned * half), span((1 - turned) * half)

    packs, held = [], []

    def hold(block, offset, cores, later):
        packs.append(block)
        held.append(Span(len(packs) - 1, 0, offset, cores, later))
        return len(packs) - 1

    def run(names, sums, is_last=False):
        return run_stage(table, queries, packs, sums, [s for s in held if s.pack in names], held, spans, is_last, packs)

    here, there = (0, 1), (1, 0)
    low_swapped, high_swapped = swap(low), swap(high)
    names = [hold(low, (0, 0), here, False), hold(low_swapped, (0, 0), there, False)]
    names += [hold(high, (0, 0), here, True), hold(high_swapped, (0, 0), there, True)]
    if size == 8:
        a = both_links(low)
        b = both_links(low_swapped)
        c = both_links(high)
        sums = run(names, None)
        a, high_swapped, sums = lax.optimization_barrier((a, high_swapped, sums))
        e = both_links(a)
        d = both_links(high_swapped)
        direct, crossed = (4, 2), (2, 4)
        names = [hold(a, direct, there, False), hold(swap(a), crossed, here, False)]
        names += [hold(b, direct, here, False), hold(swap(b), crossed, there, False)]
        sums = run(names, sums)
        c, sums = lax.optimization_barrier((c, sums))
        f = both_links(c)
        names = [hold(c, direct, there, True), hold(swap(c), crossed, here, True)]
        names += [hold(e, (6, 6), here, False), hold(swap(e), (6, 6), there, False)]
        sums = run(names, sums)
        names = [hold(d, direct, here, True), hold(swap(d), crossed, there, True)]
        sums = run(names, sums)
        f, sums = lax.optimization_barrier((f, sums))
        names = [hold(f, (6, 6), here, True), hold(swap(f), (6, 6), there, True)]
        return run(names, sums, True)
    sums = run(names, None)
    for later, block in ((False, low), (True, high)):
        got = {0: block}
        for offset in range(2, size, 2):
            step = offset & -offset
            got[offset] = swap(got[offset ^ step], step)
            names = [hold(got[offset], (offset, offset), here, later)]
            names += [hold(swap(got[offset]), (offset, offset), there, later)]
            sums = run(names, sums, later and offset == size - 2)
    return sums


def solution(mesh):
    in_specs = (P(("dp", "ctx"), None), P(("dp", "ctx"), None, None), P("dp"), P("dp"))
    out_specs = P(("dp", "ctx"), None)
    return jax.shard_map(shards, mesh=mesh, in_specs=in_specs, out_specs=out_specs, check_vma=False)
```

```python
import functools
import math

import jax
import jax.numpy as jnp
from jax import lax
from jax.experimental import pallas as pl
from jax.experimental.pallas import tpu as pltpu
from jax.sharding import PartitionSpec as P

HEADS = 32
KV_HEADS = 8
HEAD_DIM = 128
GROUP = HEADS // KV_HEADS
LOCAL_HEADS = KV_HEADS // 2
SCALE = math.log2(math.e) / math.sqrt(HEAD_DIM)
LIMIT = 2.0**90
QUERY_PIECES = 4
NT = (((1,), (1,)), ((), ()))


class Pack:
    def __init__(self, offset, other):
        self.offset, self.other = offset, other

    def places(self, fold):
        me = lax.axis_index("ctx")
        odd = me % 2
        device = me ^ (self.offset[0] + odd * (self.offset[1] - self.offset[0]) + self.other)
        return [fold[2 * device], fold[2 * device + 1]]


def prepare(q_hbm, kv_hbm, mine_ref, other_ref, *refs):
    *pieces, kv_ref, kv_sems, sems = refs
    core = lax.axis_index("ctx") % 2
    half = kv_ref.shape[0] // 2
    kv_copies = []
    for j in range(2):
        at = slice(j * half, (j + 1) * half)
        kv_copies.append(pltpu.make_async_copy(kv_hbm.at[at], kv_ref.at[at], kv_sems.at[j]))
        kv_copies[-1].start()
    rows, width = pieces[0].shape
    columns = pl.ds(pl.multiple_of((1 - core) * width, width), width)
    copies = []
    for n, piece in enumerate(pieces):
        copies.append(pltpu.make_async_copy(q_hbm.at[n * rows : (n + 1) * rows, columns], piece, sems.at[n]))
        copies[-1].start()
    width = mine_ref.shape[4]
    for j in range(2):
        kv_copies[j].wait()
        for out_ref, which in ((other_ref, 1 - core), (mine_ref, core)):
            for part in range(2):
                columns = pl.ds(pl.multiple_of((2 * which + part) * width, width), width)
                out_ref[part, j] = jnp.swapaxes(kv_ref[j * half : (j + 1) * half, :, columns], 0, 1)
    for copy in copies:
        copy.wait()


def run_prepare(queries, keys_values):
    rows, two, width = keys_values.shape
    vmem = pl.BlockSpec(memory_space=pltpu.VMEM)
    block = pltpu.VMEM((2, 2, two, rows // 2, width // 4), jnp.bfloat16)
    piece = pltpu.VMEM((rows // QUERY_PIECES, queries.shape[1] // 2), jnp.bfloat16)
    mine, other, *pieces = pl.pallas_call(
        prepare,
        out_shape=[block] * 2 + [piece] * QUERY_PIECES,
        in_specs=[pl.BlockSpec(memory_space=pl.ANY)] * 2,
        out_specs=[vmem] * (2 + QUERY_PIECES),
        scratch_shapes=[
            pltpu.VMEM((rows, two, width), jnp.bfloat16),
            pltpu.SemaphoreType.DMA((2,)),
            pltpu.SemaphoreType.DMA((QUERY_PIECES,)),
        ],
        cost_estimate=pl.CostEstimate(flops=1, bytes_accessed=1, transcendentals=0),
        name="prepare",
    )(*[pltpu.with_memory_space_constraint(x, pltpu.HBM) for x in (queries, keys_values)])
    return mine, other, pieces


def fill_table(fold, length, table):
    for n in range(fold.shape[0]):
        table[n] = fold[n]
    table[fold.shape[0]] = length[0]


def run_fill_table(fold, doc_length):
    smem = pl.BlockSpec(memory_space=pltpu.SMEM)
    return pl.pallas_call(
        fill_table,
        out_shape=pltpu.SMEM((fold.shape[0] + 1,), jnp.int32),
        in_specs=[smem, smem],
        out_specs=smem,
        cost_estimate=pl.CostEstimate(flops=1, bytes_accessed=1, transcendentals=0),
        name="fill_table",
    )(fold, doc_length)


def part_columns(core, part, width):
    return pl.ds(pl.multiple_of((2 * core + part) * width, width), width)


def place_rest(block, attended, out_hbm, sem):
    core = lax.axis_index("ctx") % 2
    copy = pltpu.make_async_copy(block, out_hbm.at[:, part_columns(1 - core, 1, block.shape[1])], sem)
    copy.start()
    copy.wait()


def run_place_rest(block, attended):
    hbm = pl.BlockSpec(memory_space=pl.ANY)
    return pl.pallas_call(
        place_rest,
        out_shape=jax.ShapeDtypeStruct(attended.shape, attended.dtype),
        in_specs=[pl.BlockSpec(memory_space=pltpu.VMEM), hbm],
        out_specs=hbm,
        scratch_shapes=[pltpu.SemaphoreType.DMA],
        input_output_aliases={1: 0},
        name="place_rest",
    )(pltpu.with_memory_space_constraint(block, pltpu.VMEM), attended)


def stage(held, every_pack, part, sides, continued, *refs):
    refs = list(refs)
    is_first, is_last = part == "first", bool(sides)
    fold = refs[0]
    if is_first:
        q_hbm, rest = refs[1], refs[2:]
        q_swapped, rest = rest[:QUERY_PIECES], rest[QUERY_PIECES:]
    else:
        q_ref, *rest = refs[1:]
    packs, rest = rest[: len(held)], rest[len(held) :]
    if not is_first:
        before, rest = rest[0], rest[1:]
    if is_last:
        every, rest = rest[: len(every_pack)], rest[len(every_pack) :]
        if continued:
            arrived, rest = rest[0], rest[2:]
        if 0 in sides:
            out_hbm, rest = rest[0], rest[1:]
        if 1 in sides:
            rest_ref, rest = rest[0], rest[1:]
        key_buf, value_buf, out_ref, worst, keys_all, values_all, out_sems, sem = rest
        if continued:
            arrived_copy = pltpu.make_async_copy(
                arrived, out_hbm.at[:, part_columns(1 - lax.axis_index("ctx") % 2, 1 - part, arrived.shape[1])], out_sems.at[2]
            )
            arrived_copy.start()
        worst[...] = jnp.ones_like(worst)
        heads = range(part * LOCAL_HEADS // 2, (part + 1) * LOCAL_HEADS // 2)
    else:
        heads = range(LOCAL_HEADS)
        if is_first:
            total, q_ref, key_buf, value_buf, q_sems = rest
        else:
            total, key_buf, value_buf = rest
    span_rows = q_ref.shape[0] // 4
    group_rows = GROUP * span_rows
    me = lax.axis_index("ctx")
    core = me % 2
    length = fold[fold.shape[0] - 1]

    if is_first:
        rows, width = q_swapped[0].shape
        columns = pl.ds(pl.multiple_of(core * width, width), width)
        own_rows = rows * QUERY_PIECES
        copies = [pltpu.make_async_copy(q_hbm.at[:, columns], q_ref.at[:own_rows], q_sems.at[QUERY_PIECES])]
        for n, piece in enumerate(q_swapped):
            at = slice(own_rows + n * rows, own_rows + (n + 1) * rows)
            copies.append(pltpu.make_async_copy(piece, q_ref.at[at], q_sems.at[n]))
        for copy in copies:
            copy.start()

    places = [place for pack in held for place in pack.places(fold)]
    for n, place in enumerate(places):
        rank = sum((other < place).astype(jnp.int32) for other in places)
        at = pl.ds(pl.multiple_of(rank * span_rows, span_rows), span_rows)
        source = packs[n // 2]
        width = source.shape[4]
        wanted = range(source.shape[0]) if not is_last or source.shape[0] == 1 else [part]
        for to, piece in enumerate(wanted):
            key_buf[at, to * width : (to + 1) * width] = source[piece, n % 2, 0]
            value_buf[at, to * width : (to + 1) * width] = source[piece, n % 2, 1]

    def query_place(i):
        return fold[2 * (me ^ (i // 2)) + i % 2]

    if is_first:
        for copy in copies:
            copy.wait()

    def column(head):
        return pl.ds(pl.multiple_of(head * HEAD_DIM, HEAD_DIM), HEAD_DIM)

    def rows_of(i):
        return pl.ds(pl.multiple_of(i * span_rows, span_rows), span_rows)

    def row_in_span():
        return lax.broadcasted_iota(jnp.int32, (group_rows, 1), 0) % span_rows

    def target_of(side):
        return rest_ref if side else out_ref

    def finish(side, i, g, place, sums):
        real = place * span_rows + row_in_span() < length
        weight_sum = sums[:, HEAD_DIM:]
        inverse = 1.0 / weight_sum
        worst[...] = jnp.maximum(worst[...], jnp.maximum(weight_sum, inverse))
        value = jnp.where(real, sums[:, :HEAD_DIM] * inverse, 0.0).astype(jnp.bfloat16)
        for n in range(GROUP):
            target_of(side)[rows_of(i - 2 * side), column((g - heads[0]) * GROUP + n)] = value[
                n * span_rows : (n + 1) * span_rows
            ]

    def add(side, i, place, seen):
        if is_first:
            col = lax.broadcasted_iota(jnp.int32, (group_rows, span_rows), 1)
            mask = col <= jnp.minimum(row_in_span(), length - 1 - place * span_rows)
        for g in heads:
            if seen:
                query = jnp.concatenate([q_ref[rows_of(i), column(g * GROUP + n)] for n in range(GROUP)], axis=0)
                keys = key_buf[: seen * span_rows, column(g - heads[0])]
                scores = lax.dot_general(query, keys, NT, preferred_element_type=jnp.float32)
                weights = jnp.exp2(scores * SCALE)
                if is_first:
                    own = jnp.where(mask, weights[:, (seen - 1) * span_rows :], 0.0)
                    parts = [weights[:, : (seen - 1) * span_rows], own]
                    weights = jnp.concatenate(parts, axis=1) if seen > 1 else own
                ones = jnp.ones((seen * span_rows, HEAD_DIM), jnp.bfloat16)
                values = jnp.concatenate([value_buf[: seen * span_rows, column(g - heads[0])], ones], axis=1)
                product = jnp.dot(weights.astype(jnp.bfloat16), values, preferred_element_type=jnp.float32)
            if is_first:
                total[i, g] = product
            elif not is_last:
                total[i, g] = before[i, g] + product
            else:
                finish(side, i, g, place, before[i, g] + product if seen else before[i, g])

    def one_span(side, i):
        place = query_place(i)
        seen = sum((other <= place).astype(jnp.int32) for other in places)
        real = place * span_rows < length

        for n in range(0 if is_last else 1, len(places) + 1):

            @pl.when(real & (seen == n))
            def _():
                add(side, i, place, n)

        if is_last:

            @pl.when(jnp.logical_not(real))
            def _():
                target = target_of(side)
                target[rows_of(i - 2 * side), :] = jnp.zeros((span_rows, target.shape[1]), jnp.bfloat16)

            if side == 0:
                out_copy(i).start()

    def out_copy(i):
        width = out_ref.shape[1]
        columns = part_columns(core, part, width)
        return pltpu.make_async_copy(out_ref.at[rows_of(i)], out_hbm.at[rows_of(i), columns], out_sems.at[i])

    if not is_last:

        def any_span(i, carry):
            one_span(None, i)
            return carry

        lax.fori_loop(0, 4, any_span, 0)
        return

    for side in sides:

        def side_span(i, carry):
            one_span(side, i)
            return carry

        lax.fori_loop(2 * side, 2 * side + 2, side_span, 0)
    if 0 in sides:
        for i in range(2):
            out_copy(i).wait()
    if continued:
        arrived_copy.wait()

    @pl.when(jnp.logical_not(jnp.max(worst[...]) < LIMIT))
    def _():
        block = 4 * span_rows

        def again(side, step, piece, inside):
            i, n = step // GROUP + 2 * side, step % GROUP
            local = piece * (LOCAL_HEADS // 2) + inside if len(heads) == LOCAL_HEADS else inside
            place = query_place(i)
            query = q_ref[rows_of(i), column((heads[0] + local) * GROUP + n)]
            row = place * span_rows + lax.broadcasted_iota(jnp.int32, (span_rows, 1), 0)

            def masked(k):
                at = pl.ds(pl.multiple_of(k * block, block), block)
                raw = SCALE * lax.dot_general(query, keys_all[at, :], NT, preferred_element_type=jnp.float32)
                key_pos = k * block + lax.broadcasted_iota(jnp.int32, (span_rows, block), 1)
                return raw, key_pos <= jnp.minimum(row, length - 1), at

            def top(k, peak):
                raw, mask, _ = masked(k)
                return jnp.maximum(peak, jnp.max(jnp.where(mask, raw, -1e30), axis=1, keepdims=True))

            blocks = place // 4 + 1
            peak = lax.fori_loop(0, blocks, top, jnp.full((span_rows, 1), -1e30, jnp.float32))

            def more(k, sums):
                raw, mask, at = masked(k)
                weights = jnp.where(mask, jnp.exp2(raw - peak), 0.0)
                product = jnp.dot(weights.astype(jnp.bfloat16), values_all[at, :], preferred_element_type=jnp.float32)
                return sums[0] + product, sums[1] + jnp.sum(weights, axis=1, keepdims=True)

            zero = (jnp.zeros((span_rows, HEAD_DIM), jnp.float32), jnp.zeros((span_rows, 1), jnp.float32))
            numerator, weight_sum = lax.fori_loop(0, blocks, more, zero)
            value = jnp.where(row < length, numerator / weight_sum, 0.0)
            target_of(side)[rows_of(i - 2 * side), column(local * GROUP + n)] = value.astype(jnp.bfloat16)

        def one_head(inside, carry):
            for pack, source in zip(every_pack, every):
                piece = part if source.shape[0] == 2 else 0
                for j, place in enumerate(pack.places(fold)):
                    for kind, target in enumerate((keys_all, values_all)):
                        copy = pltpu.make_async_copy(
                            source.at[piece, j, kind, :, column(inside)], target.at[rows_of(place), :], sem
                        )
                        copy.start()
                        copy.wait()
            for side in sides:

                def one(step, carry):
                    again(side, step, 0, inside)
                    return carry

                lax.fori_loop(0, 2 * GROUP, one, 0)
            return carry

        lax.fori_loop(0, len(heads), one_head, 0)
        if 0 in sides:
            for i in range(2):
                out_copy(i).start()
                out_copy(i).wait()


def run_stage(table, query_blocks, before, held, everything=(), part=None, sides=(), arrived=None, attended=None):
    is_first, is_last = part == "first", bool(sides)
    span_rows = held[0][1].shape[3]
    width = HEADS // 2 * HEAD_DIM
    vmem = pl.BlockSpec(memory_space=pltpu.VMEM)
    smem = pl.BlockSpec(memory_space=pltpu.SMEM)
    hbm = pl.BlockSpec(memory_space=pl.ANY)
    operands = [table, *query_blocks, *[array for _, array in held]]
    specs = [smem] + [hbm if is_first else vmem] * len(query_blocks) + [vmem] * len(held)
    sums = (4, LOCAL_HEADS, GROUP * span_rows, 2 * HEAD_DIM)
    keys = 2 * len(held) * span_rows
    heads = LOCAL_HEADS // 2 if is_last else LOCAL_HEADS
    scratch = [pltpu.VMEM((keys, heads * HEAD_DIM), jnp.bfloat16)] * 2
    aliases = {}
    if not is_first:
        operands.append(before)
        specs.append(vmem)
    if is_last:
        operands += [array for _, array in everything]
        specs += [hbm] * len(everything)
        if attended is not None:
            operands.append(pltpu.with_memory_space_constraint(arrived, pltpu.VMEM))
            specs.append(vmem)
            aliases = {len(operands): 0}
            operands.append(attended)
            specs.append(hbm)
        out_shape, out_specs = [], []
        if 0 in sides:
            out_shape.append(jax.ShapeDtypeStruct((2 * span_rows, 2 * width), jnp.bfloat16))
            out_specs.append(hbm)
        if 1 in sides:
            out_shape.append(pltpu.VMEM((2 * span_rows, width // 2), jnp.bfloat16))
            out_specs.append(vmem)
        all_keys = 2 * sum(array.shape[0] for _, array in everything if array.shape[0] == 2) // 2 * span_rows
        all_keys += 2 * sum(array.shape[0] == 1 for _, array in everything) * span_rows
        scratch = scratch + [
            pltpu.VMEM((2 * span_rows, width // 2), jnp.bfloat16),
            pltpu.VMEM((GROUP * span_rows, HEAD_DIM), jnp.float32),
            pltpu.VMEM((all_keys, HEAD_DIM), jnp.bfloat16),
            pltpu.VMEM((all_keys, HEAD_DIM), jnp.bfloat16),
            pltpu.SemaphoreType.DMA((3,)),
            pltpu.SemaphoreType.DMA,
        ]
    elif is_first:
        out_shape = [pltpu.VMEM(sums, jnp.float32), pltpu.VMEM((4 * span_rows, width), jnp.bfloat16)]
        out_specs = [vmem, vmem]
        scratch = scratch + [pltpu.SemaphoreType.DMA((QUERY_PIECES + 1,))]
    else:
        out_shape, out_specs = pltpu.VMEM(sums, jnp.float32), vmem
        aliases = {len(operands) - 1: 0}
    return pl.pallas_call(
        functools.partial(
            stage, [pack for pack, _ in held], [pack for pack, _ in everything], part, sides, attended is not None
        ),
        out_shape=out_shape,
        in_specs=specs,
        out_specs=out_specs,
        scratch_shapes=scratch,
        input_output_aliases=aliases,
        compiler_params=pltpu.CompilerParams(vmem_limit_bytes=12 << 20),
        cost_estimate=pl.CostEstimate(flops=1, bytes_accessed=1, transcendentals=0),
        name="stage",
    )(*operands)


def shards(queries, keys_values, fold, doc_length):
    size = lax.axis_size("ctx")

    def swap(name, block, mask=1):
        with jax.named_scope("swap_" + name):
            return lax.ppermute(block, "ctx", [(i, i ^ mask) for i in range(size)])

    def send(name, block, even, odd):
        with jax.named_scope("send_" + name):
            return lax.ppermute(block, "ctx", [(i, i ^ (odd if i % 2 else even)) for i in range(size)])

    mine, other, pieces = run_prepare(queries, keys_values)
    (fold, doc_length), other = lax.optimization_barrier(((fold, doc_length), other))
    table = run_fill_table(fold, doc_length)
    other = swap("kv", other)
    pieces = [swap("q", piece) for piece in pieces]
    near, far, across = (2, 4), (4, 2), (6, 6)
    held = [(Pack((0, 0), 0), mine), (Pack((0, 0), 1), other)]
    first = pltpu.with_memory_space_constraint(queries, pltpu.HBM)
    sums, query_block = run_stage(table, (first, *pieces), None, held, part="first")

    def after(items, sums):
        arrays, sums = lax.optimization_barrier(([array for _, array in items], sums))
        return [(pack, array) for (pack, _), array in zip(items, arrays)], sums

    def more(items, sums):
        return run_stage(table, (query_block,), sums, items)

    if size == 8:
        a1, b1 = send("a1", mine, 2, 4), send("b1", other, 2, 4)
        (mine, other), sums = lax.optimization_barrier(((mine, other), sums))
        a2, b2 = send("a2", mine, 4, 2), send("b2", other, 4, 2)
        (a1, b1), sums = lax.optimization_barrier(((a1, b1), sums))
        e = send("e", a1, 4, 2)
        f0, f1 = send("f0", b1[:1], 4, 2), send("f1", b1[1:], 4, 2)
        firsts = [(Pack(near, 0), a1), (Pack(near, 1), b1)]
        sums = more(firsts, sums)
        seconds, sums = after([(Pack(far, 0), a2), (Pack(far, 1), b2)], sums)
        sums = more(seconds, sums)
        e, f0, sums = lax.optimization_barrier((e, f0, sums))
        third = [(Pack(across, 0), e)]
        everything = held + firsts + seconds + third
        halves = [f0, f1]
    else:
        got = {0: (mine, other)}
        everything = list(held)
        for offset in range(2, size, 2):
            step = offset & -offset
            got[offset] = [swap("far", block, step) for block in got[offset ^ step]]
            items = [(Pack((offset, offset), n), block) for n, block in enumerate(got[offset])]
            if offset < size - 2:
                sums = more(items, sums)
                everything += items
            else:
                third = items[:1]
                everything += third
                halves = [items[1][1][:1], items[1][1][1:]]
        across = (size - 2, size - 2)
    last = [(Pack(across, 1), halves[0])]
    attended, rest0 = run_stage(table, (query_block,), sums, third + last, everything + last, 0, (0, 1))
    rest0 = swap("out0", rest0)
    halves[1], attended = lax.optimization_barrier((halves[1], attended))
    last = [(Pack(across, 1), halves[1])]
    rest1 = run_stage(table, (query_block,), sums, third + last, everything + last, 1, (1,))[0]
    rest1 = swap("out1", rest1)
    attended = run_stage(table, (query_block,), sums, third + last, everything + last, 1, (0,), rest0, attended)[0]
    return run_place_rest(rest1, attended)


def solution(mesh):
    in_specs = (P(("dp", "ctx"), None), P(("dp", "ctx"), None, None), P("dp"), P("dp"))
    out_specs = P(("dp", "ctx"), None)
    return jax.shard_map(shards, mesh=mesh, in_specs=in_specs, out_specs=out_specs, check_vma=False)
```

```python
import functools
import math

import jax
import jax.numpy as jnp
from jax import lax
from jax.experimental import pallas as pl
from jax.experimental.pallas import tpu as pltpu
from jax.sharding import PartitionSpec as P

HEADS = 32
KV_HEADS = 8
HEAD_DIM = 128
GROUP = HEADS // KV_HEADS
LOCAL_HEADS = KV_HEADS // 2
SCALE = math.log2(math.e) / math.sqrt(HEAD_DIM)
LIMIT = 2.0**90
NT = (((1,), (1,)), ((), ()))


class Pack:
    def __init__(self, offset, other):
        self.offset, self.other = offset, other

    def places(self, fold):
        me = lax.axis_index("ctx")
        odd = me % 2
        device = me ^ (self.offset[0] + odd * (self.offset[1] - self.offset[0]) + self.other)
        return [fold[2 * device], fold[2 * device + 1]]


def prepare(kv_ref, mine_ref, other_ref):
    core = lax.axis_index("ctx") % 2
    half = kv_ref.shape[0] // 2
    width = mine_ref.shape[4]
    for j in range(2):
        for out_ref, which in ((other_ref, 1 - core), (mine_ref, core)):
            for part in range(2):
                columns = pl.ds(pl.multiple_of((2 * which + part) * width, width), width)
                out_ref[part, j] = jnp.swapaxes(kv_ref[j * half : (j + 1) * half, :, columns], 0, 1)


def run_prepare(keys_values):
    rows, two, width = keys_values.shape
    vmem = pl.BlockSpec(memory_space=pltpu.VMEM)
    return pl.pallas_call(
        prepare,
        out_shape=[pltpu.VMEM((2, 2, two, rows // 2, width // 4), jnp.bfloat16)] * 2,
        in_specs=[vmem],
        out_specs=[vmem, vmem],
        cost_estimate=pl.CostEstimate(flops=1, bytes_accessed=1, transcendentals=0),
        name="prepare",
    )(keys_values)


def fill_table(fold, length, table):
    for n in range(fold.shape[0]):
        table[n] = fold[n]
    table[fold.shape[0]] = length[0]


def run_fill_table(fold, doc_length):
    smem = pl.BlockSpec(memory_space=pltpu.SMEM)
    return pl.pallas_call(
        fill_table,
        out_shape=pltpu.SMEM((fold.shape[0] + 1,), jnp.int32),
        in_specs=[smem, smem],
        out_specs=smem,
        cost_estimate=pl.CostEstimate(flops=1, bytes_accessed=1, transcendentals=0),
        name="fill_table",
    )(fold, doc_length)


def part_columns(core, part, width):
    return pl.ds(pl.multiple_of((2 * core + part) * width, width), width)


def place_rest(own, block, attended, out_hbm, sems):
    core = lax.axis_index("ctx") % 2
    copies = [
        pltpu.make_async_copy(part, out_hbm.at[:, part_columns(which, 1, part.shape[1])], sems.at[n])
        for n, (part, which) in enumerate(((own, core), (block, 1 - core)))
    ]
    for copy in copies:
        copy.start()
    for copy in copies:
        copy.wait()


def run_place_rest(own, block, attended):
    vmem = pl.BlockSpec(memory_space=pltpu.VMEM)
    hbm = pl.BlockSpec(memory_space=pl.ANY)
    return pl.pallas_call(
        place_rest,
        out_shape=jax.ShapeDtypeStruct(attended.shape, attended.dtype),
        in_specs=[vmem, vmem, hbm],
        out_specs=hbm,
        scratch_shapes=[pltpu.SemaphoreType.DMA((2,))],
        input_output_aliases={2: 0},
        name="place_rest",
    )(*[pltpu.with_memory_space_constraint(part, pltpu.VMEM) for part in (own, block)], attended)


def stage(held, every_pack, part, sides, continued, *refs):
    refs = list(refs)
    is_first, is_last = part == "first", bool(sides)
    fold = refs[0]
    if is_first:
        q_hbm, q_swapped, *rest = refs[1:]
    else:
        q_ref, *rest = refs[1:]
    packs, rest = rest[: len(held)], rest[len(held) :]
    if not is_first:
        before, rest = rest[0], rest[1:]
    if is_last:
        every, rest = rest[: len(every_pack)], rest[len(every_pack) :]
        if continued:
            arrived, rest = rest[0], rest[2:]
        if 0 in sides:
            out_hbm, rest = rest[0], rest[1:]
        if 1 in sides:
            rest_ref, rest = rest[0], rest[1:]
        if continued:
            out_ref, *rest = rest
            key_buf, value_buf, worst, keys_all, values_all, out_sems, sem = rest
        else:
            key_buf, value_buf, out_ref, worst, keys_all, values_all, out_sems, sem = rest
        if continued:
            arrived_copy = pltpu.make_async_copy(
                arrived, out_hbm.at[:, part_columns(1 - lax.axis_index("ctx") % 2, 1 - part, arrived.shape[1])], out_sems.at[2]
            )
            arrived_copy.start()
        worst[...] = jnp.ones_like(worst)
        heads = range(part * LOCAL_HEADS // 2, (part + 1) * LOCAL_HEADS // 2)
    else:
        heads = range(LOCAL_HEADS)
        if is_first:
            total, q_ref, key_buf, value_buf, q_sems = rest
        else:
            total, key_buf, value_buf = rest
    span_rows = q_ref.shape[0] // 4
    group_rows = GROUP * span_rows
    me = lax.axis_index("ctx")
    core = me % 2
    length = fold[fold.shape[0] - 1]

    if is_first:
        rows, width = q_swapped.shape[0], q_ref.shape[1]
        columns = pl.ds(pl.multiple_of(core * width, width), width)
        copies = [
            pltpu.make_async_copy(q_hbm.at[:, columns], q_ref.at[:rows], q_sems.at[0]),
            pltpu.make_async_copy(q_swapped.at[:, columns], q_ref.at[rows:], q_sems.at[1]),
        ]
        for copy in copies:
            copy.start()

    places = [place for pack in held for place in pack.places(fold)]
    for n, place in enumerate(places):
        rank = sum((other < place).astype(jnp.int32) for other in places)
        at = pl.ds(pl.multiple_of(rank * span_rows, span_rows), span_rows)
        source = packs[n // 2]
        width = source.shape[4]
        wanted = range(source.shape[0]) if not is_last or source.shape[0] == 1 else [part]
        for to, piece in enumerate(wanted):
            key_buf[at, to * width : (to + 1) * width] = source[piece, n % 2, 0]
            value_buf[at, to * width : (to + 1) * width] = source[piece, n % 2, 1]

    def query_place(i):
        return fold[2 * (me ^ (i // 2)) + i % 2]

    if is_first:
        for copy in copies:
            copy.wait()

    def column(head):
        return pl.ds(pl.multiple_of(head * HEAD_DIM, HEAD_DIM), HEAD_DIM)

    def rows_of(i):
        return pl.ds(pl.multiple_of(i * span_rows, span_rows), span_rows)

    def row_in_span():
        return lax.broadcasted_iota(jnp.int32, (group_rows, 1), 0) % span_rows

    def target_of(side):
        return rest_ref if side else out_ref

    def finish(side, i, g, real, sums):
        weight_sum = sums[:, HEAD_DIM:]
        guess = pl.reciprocal(weight_sum, approx=True)
        inverse = guess * (2.0 - weight_sum * guess)
        largest = jnp.maximum(weight_sum, guess).reshape(-1, 8, HEAD_DIM)
        worst[...] = jnp.maximum(worst[...], jnp.where(real, jnp.max(largest, axis=0), 1.0))
        value = (sums[:, :HEAD_DIM] * inverse).astype(jnp.bfloat16)
        for n in range(GROUP):
            target_of(side)[rows_of(i - 2 * side), column((g - heads[0]) * GROUP + n)] = value[
                n * span_rows : (n + 1) * span_rows
            ]

    def product_of(i, g, seen, change):
        query = jnp.concatenate([q_ref[rows_of(i), column(g * GROUP + n)] for n in range(GROUP)], axis=0)
        keys = key_buf[: seen * span_rows, column(g - heads[0])]
        scores = lax.dot_general(query, keys, NT, preferred_element_type=jnp.float32)
        weights = jnp.exp2(scores * SCALE)
        parts = [change(n, weights[:, n * span_rows : (n + 1) * span_rows]) for n in range(seen)]
        weights = jnp.concatenate(parts, axis=1) if seen > 1 else parts[0]
        ones = jnp.ones((seen * span_rows, HEAD_DIM), jnp.bfloat16)
        values = jnp.concatenate([value_buf[: seen * span_rows, column(g - heads[0])], ones], axis=1)
        return jnp.dot(weights.astype(jnp.bfloat16), values, preferred_element_type=jnp.float32)

    def add(i, place, seen):
        if is_first:
            col = lax.broadcasted_iota(jnp.int32, (group_rows, span_rows), 1)
            mask = col <= jnp.minimum(row_in_span(), length - 1 - place * span_rows)

        def change(n, weights):
            return jnp.where(mask, weights, 0.0) if is_first and n == seen - 1 else weights

        for g in heads:
            product = product_of(i, g, seen, change)
            total[i, g] = product if is_first else before[i, g] + product

    def visible_product(i, g):
        place = query_place(i)
        seen = sum((other <= place).astype(jnp.int32) for other in places)

        def change(n, weights):
            return jnp.where(seen > n, weights, 0.0)

        return product_of(i, g, len(places), change)

    def add_visible(i):
        for g in heads:
            total[i, g] = before[i, g] + visible_product(i, g)

    def add_last(side, i):
        place = query_place(i)
        real = place * span_rows < length
        for g in heads:
            finish(side, i, g, real, before[i, g] + visible_product(i, g))

        @pl.when(place * span_rows + span_rows > length)
        def _():
            target = target_of(side)
            at = rows_of(i - 2 * side)
            row = place * span_rows + lax.broadcasted_iota(jnp.int32, (span_rows, target.shape[1]), 0)
            target[at, :] = jnp.where(row < length, target[at, :].astype(jnp.float32), 0.0).astype(jnp.bfloat16)

        if side == 0 and not continued:
            out_copy(i).start()

    def any_span(i, carry):
        place = query_place(i)
        seen = sum((other <= place).astype(jnp.int32) for other in places)
        real = place * span_rows < length

        for n in range(1, len(places) + 1):

            @pl.when(real & (seen == n))
            def _():
                add(i, place, n)

        return carry

    def out_copy(i):
        width = out_ref.shape[1]
        columns = part_columns(core, part, width)
        return pltpu.make_async_copy(out_ref.at[rows_of(i)], out_hbm.at[rows_of(i), columns], out_sems.at[i])

    if not is_last:
        if is_first:
            lax.fori_loop(0, 4, any_span, 0)
            return
        if len(places) == 2:
            for i in range(4):
                add_visible(i)
            return
        lax.fori_loop(0, 4, any_span, 0)
        return
    for side in sides:
        for i in (2 * side, 2 * side + 1):
            add_last(side, i)
    if continued:
        arrived_copy.wait()
    elif 0 in sides:
        for i in range(2):
            out_copy(i).wait()

    @pl.when(jnp.logical_not(jnp.max(worst[...]) < LIMIT))
    def _():
        block = 4 * span_rows

        def again(side, step, piece, inside):
            i, n = step // GROUP + 2 * side, step % GROUP
            local = piece * (LOCAL_HEADS // 2) + inside if len(heads) == LOCAL_HEADS else inside
            place = query_place(i)
            query = q_ref[rows_of(i), column((heads[0] + local) * GROUP + n)]
            row = place * span_rows + lax.broadcasted_iota(jnp.int32, (span_rows, 1), 0)

            def masked(k):
                at = pl.ds(pl.multiple_of(k * block, block), block)
                raw = SCALE * lax.dot_general(query, keys_all[at, :], NT, preferred_element_type=jnp.float32)
                key_pos = k * block + lax.broadcasted_iota(jnp.int32, (span_rows, block), 1)
                return raw, key_pos <= jnp.minimum(row, length - 1), at

            def top(k, peak):
                raw, mask, _ = masked(k)
                return jnp.maximum(peak, jnp.max(jnp.where(mask, raw, -1e30), axis=1, keepdims=True))

            blocks = place // 4 + 1
            peak = lax.fori_loop(0, blocks, top, jnp.full((span_rows, 1), -1e30, jnp.float32))

            def more(k, sums):
                raw, mask, at = masked(k)
                weights = jnp.where(mask, jnp.exp2(raw - peak), 0.0)
                product = jnp.dot(weights.astype(jnp.bfloat16), values_all[at, :], preferred_element_type=jnp.float32)
                return sums[0] + product, sums[1] + jnp.sum(weights, axis=1, keepdims=True)

            zero = (jnp.zeros((span_rows, HEAD_DIM), jnp.float32), jnp.zeros((span_rows, 1), jnp.float32))
            numerator, weight_sum = lax.fori_loop(0, blocks, more, zero)
            value = jnp.where(row < length, numerator / weight_sum, 0.0)
            target_of(side)[rows_of(i - 2 * side), column(local * GROUP + n)] = value.astype(jnp.bfloat16)

        def one_head(inside, carry):
            for pack, source in zip(every_pack, every):
                piece = part if source.shape[0] == 2 else 0
                for j, place in enumerate(pack.places(fold)):
                    for kind, target in enumerate((keys_all, values_all)):
                        copy = pltpu.make_async_copy(
                            source.at[piece, j, kind, :, column(inside)], target.at[rows_of(place), :], sem
                        )
                        copy.start()
                        copy.wait()
            for side in sides:

                def one(step, carry):
                    again(side, step, 0, inside)
                    return carry

                lax.fori_loop(0, 2 * GROUP, one, 0)
            return carry

        lax.fori_loop(0, len(heads), one_head, 0)
        if 0 in sides and not continued:
            for i in range(2):
                out_copy(i).start()
                out_copy(i).wait()


def run_stage(table, query_blocks, before, held, everything=(), part=None, sides=(), arrived=None, attended=None):
    is_first, is_last = part == "first", bool(sides)
    span_rows = held[0][1].shape[3]
    width = HEADS // 2 * HEAD_DIM
    vmem = pl.BlockSpec(memory_space=pltpu.VMEM)
    smem = pl.BlockSpec(memory_space=pltpu.SMEM)
    hbm = pl.BlockSpec(memory_space=pl.ANY)
    operands = [table, *query_blocks, *[array for _, array in held]]
    specs = [smem] + [hbm if is_first else vmem] * len(query_blocks) + [vmem] * len(held)
    sums = (4, LOCAL_HEADS, GROUP * span_rows, 2 * HEAD_DIM)
    keys = 2 * len(held) * span_rows
    heads = LOCAL_HEADS // 2 if is_last else LOCAL_HEADS
    scratch = [pltpu.VMEM((keys, heads * HEAD_DIM), jnp.bfloat16)] * 2
    aliases = {}
    if not is_first:
        operands.append(before)
        specs.append(vmem)
    if is_last:
        operands += [array for _, array in everything]
        specs += [hbm] * len(everything)
        if attended is not None:
            operands.append(pltpu.with_memory_space_constraint(arrived, pltpu.VMEM))
            specs.append(vmem)
            aliases = {len(operands): 0}
            operands.append(attended)
            specs.append(hbm)
        out_shape, out_specs = [], []
        if 0 in sides:
            out_shape.append(jax.ShapeDtypeStruct((2 * span_rows, 2 * width), jnp.bfloat16))
            out_specs.append(hbm)
        if 1 in sides or attended is not None:
            out_shape.append(pltpu.VMEM((2 * span_rows, width // 2), jnp.bfloat16))
            out_specs.append(vmem)
        all_keys = 2 * sum(array.shape[0] for _, array in everything if array.shape[0] == 2) // 2 * span_rows
        all_keys += 2 * sum(array.shape[0] == 1 for _, array in everything) * span_rows
        if attended is None:
            scratch = scratch + [pltpu.VMEM((2 * span_rows, width // 2), jnp.bfloat16)]
        scratch = scratch + [
            pltpu.VMEM((8, HEAD_DIM), jnp.float32),
            pltpu.VMEM((all_keys, HEAD_DIM), jnp.bfloat16),
            pltpu.VMEM((all_keys, HEAD_DIM), jnp.bfloat16),
            pltpu.SemaphoreType.DMA((3,)),
            pltpu.SemaphoreType.DMA,
        ]
    elif is_first:
        out_shape = [pltpu.VMEM(sums, jnp.float32), pltpu.VMEM((4 * span_rows, width), jnp.bfloat16)]
        out_specs = [vmem, vmem]
        scratch = scratch + [pltpu.SemaphoreType.DMA((2,))]
    else:
        out_shape, out_specs = pltpu.VMEM(sums, jnp.float32), vmem
        aliases = {len(operands) - 1: 0}
    return pl.pallas_call(
        functools.partial(
            stage, [pack for pack, _ in held], [pack for pack, _ in everything], part, sides, attended is not None
        ),
        out_shape=out_shape,
        in_specs=specs,
        out_specs=out_specs,
        scratch_shapes=scratch,
        input_output_aliases=aliases,
        compiler_params=pltpu.CompilerParams(vmem_limit_bytes=12 << 20),
        cost_estimate=pl.CostEstimate(flops=1, bytes_accessed=1, transcendentals=0),
        name="stage",
    )(*operands)


def shards(queries, keys_values, fold, doc_length):
    size = lax.axis_size("ctx")

    def swap(name, block, mask=1):
        with jax.named_scope("swap_" + name):
            return lax.ppermute(block, "ctx", [(i, i ^ mask) for i in range(size)])

    def send(name, block, even, odd):
        with jax.named_scope("send_" + name):
            return lax.ppermute(block, "ctx", [(i, i ^ (odd if i % 2 else even)) for i in range(size)])

    query_other = swap("q", queries)
    mine, other = run_prepare(keys_values)
    (fold, doc_length), other = lax.optimization_barrier(((fold, doc_length), other))
    table = run_fill_table(fold, doc_length)
    other = swap("kv", other)
    near, far, across = (2, 4), (4, 2), (6, 6)
    held = [(Pack((0, 0), 0), mine), (Pack((0, 0), 1), other)]
    first = pltpu.with_memory_space_constraint(queries, pltpu.HBM)
    sums, query_block = run_stage(table, (first, query_other), None, held, part="first")

    def after(items, sums):
        arrays, sums = lax.optimization_barrier(([array for _, array in items], sums))
        return [(pack, array) for (pack, _), array in zip(items, arrays)], sums

    def more(items, sums):
        return run_stage(table, (query_block,), sums, items)

    if size == 8:
        a1, b1 = send("a1", mine, 2, 4), send("b1", other, 2, 4)
        (mine, other), sums = lax.optimization_barrier(((mine, other), sums))
        a2, b2 = send("a2", mine, 4, 2), send("b2", other, 4, 2)
        (a1, b1), sums = lax.optimization_barrier(((a1, b1), sums))
        e = send("e", a1, 4, 2)
        f0, f1 = send("f0", b1[:1], 4, 2), send("f1", b1[1:], 4, 2)
        firsts = [(Pack(near, 0), a1), (Pack(near, 1), b1)]
        sums = more(firsts, sums)
        seconds, sums = after([(Pack(far, 0), a2), (Pack(far, 1), b2)], sums)
        sums = more(seconds, sums)
        thirds, sums = after([(Pack(across, 0), e)], sums)
        sums = more(thirds, sums)
        f0, sums = lax.optimization_barrier((f0, sums))
        everything = held + firsts + seconds + thirds
        halves = [f0, f1]
    else:
        got = {0: (mine, other)}
        everything = list(held)
        for offset in range(2, size, 2):
            step = offset & -offset
            got[offset] = [swap("far", block, step) for block in got[offset ^ step]]
            items = [(Pack((offset, offset), n), block) for n, block in enumerate(got[offset])]
            if offset < size - 2:
                sums = more(items, sums)
                everything += items
            else:
                sums = more(items[:1], sums)
                everything += items[:1]
                halves = [items[1][1][:1], items[1][1][1:]]
        across = (size - 2, size - 2)
    last = [(Pack(across, 1), halves[0])]
    attended, rest0 = run_stage(table, (query_block,), sums, last, everything + last, 0, (0, 1))
    rest0 = swap("out0", rest0)
    halves[1], attended = lax.optimization_barrier((halves[1], attended))
    last = [(Pack(across, 1), halves[1])]
    rest1 = run_stage(table, (query_block,), sums, last, everything + last, 1, (1,))[0]
    rest1 = swap("out1", rest1)
    attended, own = run_stage(table, (query_block,), sums, last, everything + last, 1, (0,), rest0, attended)
    return run_place_rest(own, rest1, attended)


def solution(mesh):
    in_specs = (P(("dp", "ctx"), None), P(("dp", "ctx"), None, None), P("dp"), P("dp"))
    out_specs = P(("dp", "ctx"), None)
    return jax.shard_map(shards, mesh=mesh, in_specs=in_specs, out_specs=out_specs, check_vma=False)
```

```python
import functools
import math

import jax
import jax.numpy as jnp
from jax import lax
from jax.experimental import pallas as pl
from jax.experimental.pallas import tpu as pltpu
from jax.sharding import PartitionSpec as P

HEADS = 32
KV_HEADS = 8
HEAD_DIM = 128
GROUP = HEADS // KV_HEADS
LOCAL_HEADS = KV_HEADS // 2
SCALE = math.log2(math.e) / math.sqrt(HEAD_DIM)
LIMIT = 2.0**90
COPY_PIECES = 4
NT = (((1,), (1,)), ((), ()))


class Pack:
    def __init__(self, offset, other):
        self.offset, self.other = offset, other

    def places(self, fold):
        me = lax.axis_index("ctx")
        odd = me % 2
        device = me ^ (self.offset[0] + odd * (self.offset[1] - self.offset[0]) + self.other)
        return [fold[2 * device], fold[2 * device + 1]]


def prepare(kv_hbm, mine_ref, other_ref, kv_ref, sems):
    core = lax.axis_index("ctx") % 2
    half = kv_ref.shape[0] // 2
    rows = kv_ref.shape[0] // COPY_PIECES
    width = mine_ref.shape[4]
    copies = []
    for n in range(COPY_PIECES):
        at = slice(n * rows, (n + 1) * rows)
        copies.append(pltpu.make_async_copy(kv_hbm.at[at], kv_ref.at[at], sems.at[n]))
        copies[-1].start()
    for n in range(COPY_PIECES):
        copies[n].wait()
        j, to = n * rows // half, n * rows % half
        for out_ref, which in ((other_ref, 1 - core), (mine_ref, core)):
            for part in range(2):
                columns = pl.ds(pl.multiple_of((2 * which + part) * width, width), width)
                out_ref[part, j, :, to : to + rows] = jnp.swapaxes(kv_ref[n * rows : (n + 1) * rows, :, columns], 0, 1)


def run_prepare(keys_values):
    rows, two, width = keys_values.shape
    vmem = pl.BlockSpec(memory_space=pltpu.VMEM)
    return pl.pallas_call(
        prepare,
        out_shape=[pltpu.VMEM((2, 2, two, rows // 2, width // 4), jnp.bfloat16)] * 2,
        in_specs=[pl.BlockSpec(memory_space=pl.ANY)],
        out_specs=[vmem, vmem],
        scratch_shapes=[pltpu.VMEM((rows, two, width), jnp.bfloat16), pltpu.SemaphoreType.DMA((COPY_PIECES,))],
        cost_estimate=pl.CostEstimate(flops=1, bytes_accessed=1, transcendentals=0),
        name="prepare",
    )(pltpu.with_memory_space_constraint(keys_values, pltpu.HBM))


def fill_table(fold, length, table):
    for n in range(fold.shape[0]):
        table[n] = fold[n]
    table[fold.shape[0]] = length[0]


def run_fill_table(fold, doc_length):
    smem = pl.BlockSpec(memory_space=pltpu.SMEM)
    return pl.pallas_call(
        fill_table,
        out_shape=pltpu.SMEM((fold.shape[0] + 1,), jnp.int32),
        in_specs=[smem, smem],
        out_specs=smem,
        cost_estimate=pl.CostEstimate(flops=1, bytes_accessed=1, transcendentals=0),
        name="fill_table",
    )(fold, doc_length)


def part_columns(core, part, width):
    return pl.ds(pl.multiple_of((2 * core + part) * width, width), width)


def row_pieces(block, target, columns, sems):
    rows = block.shape[0] // COPY_PIECES
    pieces = [slice(n * rows, (n + 1) * rows) for n in range(COPY_PIECES)]
    return [pltpu.make_async_copy(block.at[at], target.at[at, columns], sems.at[n]) for n, at in enumerate(pieces)]


def place_rest(own, block, attended, out_hbm, sems):
    core = lax.axis_index("ctx") % 2
    copies = []
    for n, (part, which) in enumerate(((own, core), (block, 1 - core))):
        copies += row_pieces(part, out_hbm, part_columns(which, 1, part.shape[1]), sems.at[n])
    for copy in copies:
        copy.start()
    for copy in copies:
        copy.wait()


def run_place_rest(own, block, attended):
    vmem = pl.BlockSpec(memory_space=pltpu.VMEM)
    hbm = pl.BlockSpec(memory_space=pl.ANY)
    return pl.pallas_call(
        place_rest,
        out_shape=jax.ShapeDtypeStruct(attended.shape, attended.dtype),
        in_specs=[vmem, vmem, hbm],
        out_specs=hbm,
        scratch_shapes=[pltpu.SemaphoreType.DMA((2, COPY_PIECES))],
        input_output_aliases={2: 0},
        name="place_rest",
    )(*[pltpu.with_memory_space_constraint(part, pltpu.VMEM) for part in (own, block)], attended)


def stage(held, every_pack, part, sides, continued, *refs):
    refs = list(refs)
    is_first, is_last = part == "first", bool(sides)
    fold = refs[0]
    if is_first:
        q_hbm, q_swapped, *rest = refs[1:]
    else:
        q_ref, *rest = refs[1:]
    packs, rest = rest[: len(held)], rest[len(held) :]
    if not is_first:
        before, rest = rest[0], rest[1:]
    if is_last:
        every, rest = rest[: len(every_pack)], rest[len(every_pack) :]
        if continued:
            arrived, rest = rest[0], rest[2:]
        if 0 in sides:
            out_hbm, rest = rest[0], rest[1:]
        if 1 in sides:
            rest_ref, rest = rest[0], rest[1:]
        if continued:
            out_ref, *rest = rest
            key_buf, value_buf, worst, keys_all, values_all, out_sems, sem = rest
        else:
            key_buf, value_buf, out_ref, worst, keys_all, values_all, out_sems, sem = rest
        if continued:
            columns = part_columns(1 - lax.axis_index("ctx") % 2, 1 - part, arrived.shape[1])
            arrived_copies = row_pieces(arrived, out_hbm, columns, out_sems)
            for copy in arrived_copies:
                copy.start()
        worst[...] = jnp.ones_like(worst)
        heads = range(part * LOCAL_HEADS // 2, (part + 1) * LOCAL_HEADS // 2)
    else:
        heads = range(LOCAL_HEADS)
        if is_first:
            total, q_ref, key_buf, value_buf, q_sems = rest
        else:
            total, key_buf, value_buf = rest
    span_rows = q_ref.shape[0] // 4
    group_rows = GROUP * span_rows
    spans = fold.shape[0]
    me = lax.axis_index("ctx")
    core = me % 2
    length = fold[fold.shape[0] - 1]

    if is_first:
        half, width = q_swapped.shape[0] // 2, q_ref.shape[1]
        columns = pl.ds(pl.multiple_of(core * width, width), width)
        copies = [
            pltpu.make_async_copy(
                source.at[j * half : (j + 1) * half, columns],
                q_ref.at[(2 * n + j) * half : (2 * n + j + 1) * half],
                q_sems.at[2 * n + j],
            )
            for n, source in enumerate((q_hbm, q_swapped))
            for j in range(2)
        ]
        for copy in copies:
            copy.start()

    places = [place for pack in held for place in pack.places(fold)]
    for n, place in enumerate(places):
        rank = sum((other < place).astype(jnp.int32) for other in places)
        at = pl.ds(pl.multiple_of(rank * span_rows, span_rows), span_rows)
        source = packs[n // 2]
        width = source.shape[4]
        wanted = range(source.shape[0]) if not is_last or source.shape[0] == 1 else [part]
        for to, piece in enumerate(wanted):
            key_buf[at, to * width : (to + 1) * width] = source[piece, n % 2, 0]
            value_buf[at, to * width : (to + 1) * width] = source[piece, n % 2, 1]

    def query_place(i):
        return fold[2 * (me ^ (i // 2)) + i % 2]

    def column(head):
        return pl.ds(pl.multiple_of(head * HEAD_DIM, HEAD_DIM), HEAD_DIM)

    def rows_of(i):
        return pl.ds(pl.multiple_of(i * span_rows, span_rows), span_rows)

    def row_in_span():
        return lax.broadcasted_iota(jnp.int32, (group_rows, 1), 0) % span_rows

    def target_of(side):
        return rest_ref if side else out_ref

    def finish(side, i, g, real, sums):
        weight_sum = sums[:, HEAD_DIM:]
        guess = pl.reciprocal(weight_sum, approx=True)
        inverse = guess * (2.0 - weight_sum * guess)
        largest = jnp.maximum(weight_sum, guess).reshape(-1, 8, HEAD_DIM)
        worst[...] = jnp.maximum(worst[...], jnp.where(real, jnp.max(largest, axis=0), 1.0))
        value = (sums[:, :HEAD_DIM] * inverse).astype(jnp.bfloat16)
        for n in range(GROUP):
            target_of(side)[rows_of(i - 2 * side), column((g - heads[0]) * GROUP + n)] = value[
                n * span_rows : (n + 1) * span_rows
            ]

    def product_of(i, g, seen, change):
        query = jnp.concatenate([q_ref[rows_of(i), column(g * GROUP + n)] for n in range(GROUP)], axis=0)
        keys = key_buf[: seen * span_rows, column(g - heads[0])]
        scores = lax.dot_general(query, keys, NT, preferred_element_type=jnp.float32)
        weights = jnp.exp2(scores * SCALE)
        parts = [change(n, weights[:, n * span_rows : (n + 1) * span_rows]) for n in range(seen)]
        weights = jnp.concatenate(parts, axis=1) if seen > 1 else parts[0]
        ones = jnp.ones((seen * span_rows, HEAD_DIM), jnp.bfloat16)
        values = jnp.concatenate([value_buf[: seen * span_rows, column(g - heads[0])], ones], axis=1)
        return jnp.dot(weights.astype(jnp.bfloat16), values, preferred_element_type=jnp.float32)

    def visible_product(i, g):
        place = query_place(i)
        seen = sum((other <= place).astype(jnp.int32) for other in places)

        def change(n, weights):
            if not is_first:
                return jnp.where(seen > n, weights, 0.0)
            col = lax.broadcasted_iota(jnp.int32, (group_rows, span_rows), 1)
            slack = jnp.minimum(row_in_span(), length - 1 - place * span_rows) - col
            least = jnp.where(n == seen - 1, 0, jnp.where(n < seen, -2 * span_rows * spans, 2 * span_rows * spans))
            return jnp.where(slack >= least, weights, 0.0)

        return product_of(i, g, len(places), change)

    def add(i):
        for g in heads:
            total[i, g] = visible_product(i, g) if is_first else total[i, g] + visible_product(i, g)

    def add_last(side):
        for i in (2 * side, 2 * side + 1):
            for g in heads:
                finish(side, i, g, query_place(i) * span_rows < length, before[i, g] + visible_product(i, g))
        ends = [query_place(i) * span_rows + span_rows for i in (2 * side, 2 * side + 1)]

        @pl.when(jnp.maximum(ends[0], ends[1]) > length)
        def _():
            target = target_of(side)
            for i, end in enumerate(ends):
                row = end - span_rows + lax.broadcasted_iota(jnp.int32, (span_rows, target.shape[1]), 0)
                kept = jnp.where(row < length, target[rows_of(i), :].astype(jnp.float32), 0.0)
                target[rows_of(i), :] = kept.astype(jnp.bfloat16)

        if side == 0 and not continued:
            for i in range(2):
                out_copy(i).start()

    def out_copy(i):
        width = out_ref.shape[1]
        columns = part_columns(core, part, width)
        return pltpu.make_async_copy(out_ref.at[rows_of(i)], out_hbm.at[rows_of(i), columns], out_sems.at[i])

    if not is_last:
        for i in range(4):
            if is_first:
                copies[i].wait()
            add(i)
        return
    for side in sides:
        add_last(side)
    if continued:
        for copy in arrived_copies:
            copy.wait()
    elif 0 in sides:
        for i in range(2):
            out_copy(i).wait()

    @pl.when(jnp.logical_not(jnp.max(worst[...]) < LIMIT))
    def _():
        block = 4 * span_rows

        def again(side, step, piece, inside):
            i, n = step // GROUP + 2 * side, step % GROUP
            local = piece * (LOCAL_HEADS // 2) + inside if len(heads) == LOCAL_HEADS else inside
            place = query_place(i)
            query = q_ref[rows_of(i), column((heads[0] + local) * GROUP + n)]
            row = place * span_rows + lax.broadcasted_iota(jnp.int32, (span_rows, 1), 0)

            def masked(k):
                at = pl.ds(pl.multiple_of(k * block, block), block)
                raw = SCALE * lax.dot_general(query, keys_all[at, :], NT, preferred_element_type=jnp.float32)
                key_pos = k * block + lax.broadcasted_iota(jnp.int32, (span_rows, block), 1)
                return raw, key_pos <= jnp.minimum(row, length - 1), at

            def top(k, peak):
                raw, mask, _ = masked(k)
                return jnp.maximum(peak, jnp.max(jnp.where(mask, raw, -1e30), axis=1, keepdims=True))

            blocks = place // 4 + 1
            peak = lax.fori_loop(0, blocks, top, jnp.full((span_rows, 1), -1e30, jnp.float32))

            def more(k, sums):
                raw, mask, at = masked(k)
                weights = jnp.where(mask, jnp.exp2(raw - peak), 0.0)
                product = jnp.dot(weights.astype(jnp.bfloat16), values_all[at, :], preferred_element_type=jnp.float32)
                return sums[0] + product, sums[1] + jnp.sum(weights, axis=1, keepdims=True)

            zero = (jnp.zeros((span_rows, HEAD_DIM), jnp.float32), jnp.zeros((span_rows, 1), jnp.float32))
            numerator, weight_sum = lax.fori_loop(0, blocks, more, zero)
            value = jnp.where(row < length, numerator / weight_sum, 0.0)
            target_of(side)[rows_of(i - 2 * side), column(local * GROUP + n)] = value.astype(jnp.bfloat16)

        def one_head(inside, carry):
            for pack, source in zip(every_pack, every):
                piece = part if source.shape[0] == 2 else 0
                for j, place in enumerate(pack.places(fold)):
                    for kind, target in enumerate((keys_all, values_all)):
                        copy = pltpu.make_async_copy(
                            source.at[piece, j, kind, :, column(inside)], target.at[rows_of(place), :], sem
                        )
                        copy.start()
                        copy.wait()
            for side in sides:

                def one(step, carry):
                    again(side, step, 0, inside)
                    return carry

                lax.fori_loop(0, 2 * GROUP, one, 0)
            return carry

        lax.fori_loop(0, len(heads), one_head, 0)
        if 0 in sides and not continued:
            for i in range(2):
                out_copy(i).start()
                out_copy(i).wait()


def run_stage(table, query_blocks, before, held, everything=(), part=None, sides=(), arrived=None, attended=None):
    is_first, is_last = part == "first", bool(sides)
    span_rows = held[0][1].shape[3]
    width = HEADS // 2 * HEAD_DIM
    vmem = pl.BlockSpec(memory_space=pltpu.VMEM)
    smem = pl.BlockSpec(memory_space=pltpu.SMEM)
    hbm = pl.BlockSpec(memory_space=pl.ANY)
    operands = [table, *query_blocks, *[array for _, array in held]]
    specs = [smem] + [hbm if is_first else vmem] * len(query_blocks) + [vmem] * len(held)
    sums = (4, LOCAL_HEADS, GROUP * span_rows, 2 * HEAD_DIM)
    keys = 2 * len(held) * span_rows
    heads = LOCAL_HEADS // 2 if is_last else LOCAL_HEADS
    scratch = [pltpu.VMEM((keys, heads * HEAD_DIM), jnp.bfloat16)] * 2
    aliases = {}
    if not is_first:
        operands.append(before)
        specs.append(vmem)
    if is_last:
        operands += [array for _, array in everything]
        specs += [hbm] * len(everything)
        if attended is not None:
            operands.append(pltpu.with_memory_space_constraint(arrived, pltpu.VMEM))
            specs.append(vmem)
            aliases = {len(operands): 0}
            operands.append(attended)
            specs.append(hbm)
        out_shape, out_specs = [], []
        if 0 in sides:
            out_shape.append(jax.ShapeDtypeStruct((2 * span_rows, 2 * width), jnp.bfloat16))
            out_specs.append(hbm)
        if 1 in sides or attended is not None:
            out_shape.append(pltpu.VMEM((2 * span_rows, width // 2), jnp.bfloat16))
            out_specs.append(vmem)
        all_keys = 2 * sum(array.shape[0] for _, array in everything if array.shape[0] == 2) // 2 * span_rows
        all_keys += 2 * sum(array.shape[0] == 1 for _, array in everything) * span_rows
        if attended is None:
            scratch = scratch + [pltpu.VMEM((2 * span_rows, width // 2), jnp.bfloat16)]
        scratch = scratch + [
            pltpu.VMEM((8, HEAD_DIM), jnp.float32),
            pltpu.VMEM((all_keys, HEAD_DIM), jnp.bfloat16),
            pltpu.VMEM((all_keys, HEAD_DIM), jnp.bfloat16),
            pltpu.SemaphoreType.DMA((COPY_PIECES,)),
            pltpu.SemaphoreType.DMA,
        ]
    elif is_first:
        out_shape = [pltpu.VMEM(sums, jnp.float32), pltpu.VMEM((4 * span_rows, width), jnp.bfloat16)]
        out_specs = [vmem, vmem]
        scratch = scratch + [pltpu.SemaphoreType.DMA((4,))]
    else:
        out_shape, out_specs = pltpu.VMEM(sums, jnp.float32), vmem
        aliases = {len(operands) - 1: 0}
    return pl.pallas_call(
        functools.partial(
            stage, [pack for pack, _ in held], [pack for pack, _ in everything], part, sides, attended is not None
        ),
        out_shape=out_shape,
        in_specs=specs,
        out_specs=out_specs,
        scratch_shapes=scratch,
        input_output_aliases=aliases,
        compiler_params=pltpu.CompilerParams(vmem_limit_bytes=12 << 20),
        cost_estimate=pl.CostEstimate(flops=1, bytes_accessed=1, transcendentals=0),
        name="stage",
    )(*operands)


def shards(queries, keys_values, fold, doc_length):
    size = lax.axis_size("ctx")

    def swap(name, block, mask=1):
        with jax.named_scope("swap_" + name):
            return lax.ppermute(block, "ctx", [(i, i ^ mask) for i in range(size)])

    def send(name, block, even, odd):
        with jax.named_scope("send_" + name):
            return lax.ppermute(block, "ctx", [(i, i ^ (odd if i % 2 else even)) for i in range(size)])

    query_other = swap("q", queries)
    mine, other = run_prepare(keys_values)
    (fold, doc_length), other = lax.optimization_barrier(((fold, doc_length), other))
    other = swap("kv", other)
    table, other = lax.optimization_barrier((run_fill_table(fold, doc_length), other))
    near, far, across = (2, 4), (4, 2), (6, 6)
    held = [(Pack((0, 0), 0), mine), (Pack((0, 0), 1), other)]
    first = pltpu.with_memory_space_constraint(queries, pltpu.HBM)
    sums, query_block = run_stage(table, (first, query_other), None, held, part="first")

    def after(items, sums):
        arrays, sums = lax.optimization_barrier(([array for _, array in items], sums))
        return [(pack, array) for (pack, _), array in zip(items, arrays)], sums

    def more(items, sums):
        return run_stage(table, (query_block,), sums, items)

    if size == 8:
        a1, b1 = send("a1", mine, 2, 4), send("b1", other, 2, 4)
        (mine, other), sums = lax.optimization_barrier(((mine, other), sums))
        a2, b2 = send("a2", mine, 4, 2), send("b2", other, 4, 2)
        (a1, b1), sums = lax.optimization_barrier(((a1, b1), sums))
        e = send("e", a1, 4, 2)
        f0, f1 = send("f0", b1[:1], 4, 2), send("f1", b1[1:], 4, 2)
        firsts = [(Pack(near, 0), a1), (Pack(near, 1), b1)]
        sums = more(firsts, sums)
        seconds, sums = after([(Pack(far, 0), a2), (Pack(far, 1), b2)], sums)
        sums = more(seconds, sums)
        thirds, sums = after([(Pack(across, 0), e)], sums)
        sums = more(thirds, sums)
        f0, sums = lax.optimization_barrier((f0, sums))
        everything = held + firsts + seconds + thirds
        halves = [f0, f1]
    else:
        got = {0: (mine, other)}
        everything = list(held)
        for offset in range(2, size, 2):
            step = offset & -offset
            got[offset] = [swap("far", block, step) for block in got[offset ^ step]]
            items = [(Pack((offset, offset), n), block) for n, block in enumerate(got[offset])]
            if offset < size - 2:
                sums = more(items, sums)
                everything += items
            else:
                sums = more(items[:1], sums)
                everything += items[:1]
                halves = [items[1][1][:1], items[1][1][1:]]
        across = (size - 2, size - 2)
    last = [(Pack(across, 1), halves[0])]
    attended, rest0 = run_stage(table, (query_block,), sums, last, everything + last, 0, (0, 1))
    rest0 = swap("out0", rest0)
    halves[1], attended = lax.optimization_barrier((halves[1], attended))
    last = [(Pack(across, 1), halves[1])]
    rest1 = run_stage(table, (query_block,), sums, last, everything + last, 1, (1,))[0]
    rest1 = swap("out1", rest1)
    attended, own = run_stage(table, (query_block,), sums, last, everything + last, 1, (0,), rest0, attended)
    return run_place_rest(own, rest1, attended)


def solution(mesh):
    in_specs = (P(("dp", "ctx"), None), P(("dp", "ctx"), None, None), P("dp"), P("dp"))
    out_specs = P(("dp", "ctx"), None)
    return jax.shard_map(shards, mesh=mesh, in_specs=in_specs, out_specs=out_specs, check_vma=False)
```

```python
import functools
import math

import jax
import jax.numpy as jnp
from jax import lax
from jax.experimental import pallas as pl
from jax.experimental.pallas import tpu as pltpu
from jax.sharding import PartitionSpec as P

HEADS = 32
KV_HEADS = 8
HEAD_DIM = 128
GROUP = HEADS // KV_HEADS
LOCAL_HEADS = KV_HEADS // 2
SCALE = math.log2(math.e) / math.sqrt(HEAD_DIM)
LIMIT = 2.0**90
COPY_PIECES = 4
NT = (((1,), (1,)), ((), ()))


class Pack:
    def __init__(self, offset, other):
        self.offset, self.other = offset, other

    def places(self, fold):
        me = lax.axis_index("ctx")
        odd = me % 2
        device = me ^ (self.offset[0] + odd * (self.offset[1] - self.offset[0]) + self.other)
        return [fold[2 * device], fold[2 * device + 1]]


def prepare(kv_hbm, mine_ref, other_ref, kv_ref, sems):
    core = lax.axis_index("ctx") % 2
    half = kv_ref.shape[0] // 2
    rows = kv_ref.shape[0] // COPY_PIECES
    width = mine_ref.shape[4]
    copies = []
    for n in range(COPY_PIECES):
        at = slice(n * rows, (n + 1) * rows)
        copies.append(pltpu.make_async_copy(kv_hbm.at[at], kv_ref.at[at], sems.at[n]))
        copies[-1].start()
    for n in range(COPY_PIECES):
        copies[n].wait()
        j, to = n * rows // half, n * rows % half
        for out_ref, which in ((other_ref, 1 - core), (mine_ref, core)):
            for part in range(2):
                columns = pl.ds(pl.multiple_of((2 * which + part) * width, width), width)
                out_ref[part, j, :, to : to + rows] = jnp.swapaxes(kv_ref[n * rows : (n + 1) * rows, :, columns], 0, 1)


def run_prepare(keys_values):
    rows, two, width = keys_values.shape
    vmem = pl.BlockSpec(memory_space=pltpu.VMEM)
    return pl.pallas_call(
        prepare,
        out_shape=[pltpu.VMEM((2, 2, two, rows // 2, width // 4), jnp.bfloat16)] * 2,
        in_specs=[pl.BlockSpec(memory_space=pl.ANY)],
        out_specs=[vmem, vmem],
        scratch_shapes=[pltpu.VMEM((rows, two, width), jnp.bfloat16), pltpu.SemaphoreType.DMA((COPY_PIECES,))],
        cost_estimate=pl.CostEstimate(flops=1, bytes_accessed=1, transcendentals=0),
        name="prepare",
    )(pltpu.with_memory_space_constraint(keys_values, pltpu.HBM))


def fill_table(fold, length, table):
    for n in range(fold.shape[0]):
        table[n] = fold[n]
    table[fold.shape[0]] = length[0]


def run_fill_table(fold, doc_length):
    smem = pl.BlockSpec(memory_space=pltpu.SMEM)
    return pl.pallas_call(
        fill_table,
        out_shape=pltpu.SMEM((fold.shape[0] + 1,), jnp.int32),
        in_specs=[smem, smem],
        out_specs=smem,
        cost_estimate=pl.CostEstimate(flops=1, bytes_accessed=1, transcendentals=0),
        name="fill_table",
    )(fold, doc_length)


def part_columns(core, part, width):
    return pl.ds(pl.multiple_of((2 * core + part) * width, width), width)


def place_rest(own, block0, block1, attended, out_hbm, sems):
    core = lax.axis_index("ctx") % 2
    pieces = ((own, core, 1), (block1, 1 - core, 1), (block0, 1 - core, 0))
    copies = [
        pltpu.make_async_copy(piece, out_hbm.at[:, part_columns(which, part, piece.shape[1])], sems.at[n])
        for n, (piece, which, part) in enumerate(pieces)
    ]
    for copy in copies:
        copy.start()
    for copy in copies:
        copy.wait()


def run_place_rest(own, block0, block1, attended):
    vmem = pl.BlockSpec(memory_space=pltpu.VMEM)
    hbm = pl.BlockSpec(memory_space=pl.ANY)
    return pl.pallas_call(
        place_rest,
        out_shape=jax.ShapeDtypeStruct(attended.shape, attended.dtype),
        in_specs=[vmem, vmem, vmem, hbm],
        out_specs=hbm,
        scratch_shapes=[pltpu.SemaphoreType.DMA((3,))],
        input_output_aliases={3: 0},
        compiler_params=pltpu.CompilerParams(vmem_limit_bytes=4 << 20),
        name="place_rest",
    )(*[pltpu.with_memory_space_constraint(part, pltpu.VMEM) for part in (own, block0, block1)], attended)


def stage(held, every_pack, part, sides, continued, *refs):
    refs = list(refs)
    is_first, is_last = part == "first", bool(sides)
    fold = refs[0]
    if is_first:
        q_hbm, q_swapped, *rest = refs[1:]
    else:
        q_ref, *rest = refs[1:]
    packs, rest = rest[: len(held)], rest[len(held) :]
    if not is_first:
        before, rest = rest[0], rest[1:]
    if is_last:
        every, rest = rest[: len(every_pack)], rest[len(every_pack) :]
        if 0 in sides and not continued:
            out_hbm, rest = rest[0], rest[1:]
        if 1 in sides:
            rest_ref, rest = rest[0], rest[1:]
        if continued:
            out_ref, *rest = rest
            key_buf, value_buf, worst, keys_all, values_all, out_sems, sem = rest
        else:
            key_buf, value_buf, out_ref, worst, keys_all, values_all, out_sems, sem = rest
        worst[...] = jnp.ones_like(worst)
        heads = range(part * LOCAL_HEADS // 2, (part + 1) * LOCAL_HEADS // 2)
    else:
        heads = range(LOCAL_HEADS)
        if is_first:
            total, q_ref, key_buf, value_buf, q_sems = rest
        else:
            total, key_buf, value_buf = rest
    span_rows = q_ref.shape[0] // 4
    group_rows = GROUP * span_rows
    spans = fold.shape[0]
    me = lax.axis_index("ctx")
    core = me % 2
    length = fold[fold.shape[0] - 1]

    if is_first:
        half, width = q_swapped.shape[0] // 2, q_ref.shape[1]
        columns = pl.ds(pl.multiple_of(core * width, width), width)
        copies = [
            pltpu.make_async_copy(
                source.at[j * half : (j + 1) * half, columns],
                q_ref.at[(2 * n + j) * half : (2 * n + j + 1) * half],
                q_sems.at[2 * n + j],
            )
            for n, source in enumerate((q_hbm, q_swapped))
            for j in range(2)
        ]
        for copy in copies:
            copy.start()

    places = [place for pack in held for place in pack.places(fold)]
    for n, place in enumerate(places):
        rank = sum((other < place).astype(jnp.int32) for other in places)
        at = pl.ds(pl.multiple_of(rank * span_rows, span_rows), span_rows)
        source = packs[n // 2]
        width = source.shape[4]
        wanted = range(source.shape[0]) if not is_last or source.shape[0] == 1 else [part]
        for to, piece in enumerate(wanted):
            key_buf[at, to * width : (to + 1) * width] = source[piece, n % 2, 0]
            value_buf[at, to * width : (to + 1) * width] = source[piece, n % 2, 1]

    def query_place(i):
        return fold[2 * (me ^ (i // 2)) + i % 2]

    def column(head):
        return pl.ds(pl.multiple_of(head * HEAD_DIM, HEAD_DIM), HEAD_DIM)

    def rows_of(i):
        return pl.ds(pl.multiple_of(i * span_rows, span_rows), span_rows)

    def row_in_span():
        return lax.broadcasted_iota(jnp.int32, (group_rows, 1), 0) % span_rows

    def target_of(side):
        return rest_ref if side else out_ref

    def finish(side, i, g, real, sums):
        weight_sum = sums[:, HEAD_DIM:]
        guess = pl.reciprocal(weight_sum, approx=True)
        inverse = guess * (2.0 - weight_sum * guess)
        largest = jnp.maximum(weight_sum, guess).reshape(-1, 8, HEAD_DIM)
        worst[...] = jnp.maximum(worst[...], jnp.where(real, jnp.max(largest, axis=0), 1.0))
        value = (sums[:, :HEAD_DIM] * inverse).astype(jnp.bfloat16)
        for n in range(GROUP):
            target_of(side)[rows_of(i - 2 * side), column((g - heads[0]) * GROUP + n)] = value[
                n * span_rows : (n + 1) * span_rows
            ]

    def product_of(i, g, seen, change):
        query = jnp.concatenate([q_ref[rows_of(i), column(g * GROUP + n)] for n in range(GROUP)], axis=0)
        keys = key_buf[: seen * span_rows, column(g - heads[0])]
        scores = lax.dot_general(query, keys, NT, preferred_element_type=jnp.float32)
        weights = jnp.exp2(scores * SCALE)
        parts = [change(n, weights[:, n * span_rows : (n + 1) * span_rows]) for n in range(seen)]
        weights = jnp.concatenate(parts, axis=1) if seen > 1 else parts[0]
        ones = jnp.ones((seen * span_rows, HEAD_DIM), jnp.bfloat16)
        values = jnp.concatenate([value_buf[: seen * span_rows, column(g - heads[0])], ones], axis=1)
        return jnp.dot(weights.astype(jnp.bfloat16), values, preferred_element_type=jnp.float32)

    def visible_product(i, g):
        place = query_place(i)
        seen = sum((other <= place).astype(jnp.int32) for other in places)

        def change(n, weights):
            if not is_first:
                return jnp.where(seen > n, weights, 0.0)
            col = lax.broadcasted_iota(jnp.int32, (group_rows, span_rows), 1)
            slack = jnp.minimum(row_in_span(), length - 1 - place * span_rows) - col
            least = jnp.where(n == seen - 1, 0, jnp.where(n < seen, -2 * span_rows * spans, 2 * span_rows * spans))
            return jnp.where(slack >= least, weights, 0.0)

        return product_of(i, g, len(places), change)

    def add(i):
        for g in heads:
            total[i, g] = visible_product(i, g) if is_first else total[i, g] + visible_product(i, g)

    def add_last(side):
        for i in (2 * side, 2 * side + 1):
            for g in heads:
                finish(side, i, g, query_place(i) * span_rows < length, before[i, g] + visible_product(i, g))
        ends = [query_place(i) * span_rows + span_rows for i in (2 * side, 2 * side + 1)]

        @pl.when(jnp.maximum(ends[0], ends[1]) > length)
        def _():
            target = target_of(side)
            for i, end in enumerate(ends):
                row = end - span_rows + lax.broadcasted_iota(jnp.int32, (span_rows, target.shape[1]), 0)
                kept = jnp.where(row < length, target[rows_of(i), :].astype(jnp.float32), 0.0)
                target[rows_of(i), :] = kept.astype(jnp.bfloat16)

        if side == 0 and not continued:
            for i in range(2):
                out_copy(i).start()

    def out_copy(i):
        width = out_ref.shape[1]
        columns = part_columns(core, part, width)
        return pltpu.make_async_copy(out_ref.at[rows_of(i)], out_hbm.at[rows_of(i), columns], out_sems.at[i])

    if not is_last:
        for i in range(4):
            if is_first:
                copies[i].wait()
            add(i)
        return
    for side in sides:
        add_last(side)
    if 0 in sides and not continued:
        for i in range(2):
            out_copy(i).wait()

    @pl.when(jnp.logical_not(jnp.max(worst[...]) < LIMIT))
    def _():
        block = 4 * span_rows

        def again(side, step, piece, inside):
            i, n = step // GROUP + 2 * side, step % GROUP
            local = piece * (LOCAL_HEADS // 2) + inside if len(heads) == LOCAL_HEADS else inside
            place = query_place(i)
            query = q_ref[rows_of(i), column((heads[0] + local) * GROUP + n)]
            row = place * span_rows + lax.broadcasted_iota(jnp.int32, (span_rows, 1), 0)

            def masked(k):
                at = pl.ds(pl.multiple_of(k * block, block), block)
                raw = SCALE * lax.dot_general(query, keys_all[at, :], NT, preferred_element_type=jnp.float32)
                key_pos = k * block + lax.broadcasted_iota(jnp.int32, (span_rows, block), 1)
                return raw, key_pos <= jnp.minimum(row, length - 1), at

            def top(k, peak):
                raw, mask, _ = masked(k)
                return jnp.maximum(peak, jnp.max(jnp.where(mask, raw, -1e30), axis=1, keepdims=True))

            blocks = place // 4 + 1
            peak = lax.fori_loop(0, blocks, top, jnp.full((span_rows, 1), -1e30, jnp.float32))

            def more(k, sums):
                raw, mask, at = masked(k)
                weights = jnp.where(mask, jnp.exp2(raw - peak), 0.0)
                product = jnp.dot(weights.astype(jnp.bfloat16), values_all[at, :], preferred_element_type=jnp.float32)
                return sums[0] + product, sums[1] + jnp.sum(weights, axis=1, keepdims=True)

            zero = (jnp.zeros((span_rows, HEAD_DIM), jnp.float32), jnp.zeros((span_rows, 1), jnp.float32))
            numerator, weight_sum = lax.fori_loop(0, blocks, more, zero)
            value = jnp.where(row < length, numerator / weight_sum, 0.0)
            target_of(side)[rows_of(i - 2 * side), column(local * GROUP + n)] = value.astype(jnp.bfloat16)

        def one_head(inside, carry):
            for pack, source in zip(every_pack, every):
                piece = part if source.shape[0] == 2 else 0
                for j, place in enumerate(pack.places(fold)):
                    for kind, target in enumerate((keys_all, values_all)):
                        copy = pltpu.make_async_copy(
                            source.at[piece, j, kind, :, column(inside)], target.at[rows_of(place), :], sem
                        )
                        copy.start()
                        copy.wait()
            for side in sides:

                def one(step, carry):
                    again(side, step, 0, inside)
                    return carry

                lax.fori_loop(0, 2 * GROUP, one, 0)
            return carry

        lax.fori_loop(0, len(heads), one_head, 0)
        if 0 in sides and not continued:
            for i in range(2):
                out_copy(i).start()
                out_copy(i).wait()


def run_stage(table, query_blocks, before, held, everything=(), part=None, sides=(), continued=False):
    is_first, is_last = part == "first", bool(sides)
    span_rows = held[0][1].shape[3]
    width = HEADS // 2 * HEAD_DIM
    vmem = pl.BlockSpec(memory_space=pltpu.VMEM)
    smem = pl.BlockSpec(memory_space=pltpu.SMEM)
    hbm = pl.BlockSpec(memory_space=pl.ANY)
    operands = [table, *query_blocks, *[array for _, array in held]]
    specs = [smem] + [hbm if is_first else vmem] * len(query_blocks) + [vmem] * len(held)
    sums = (4, LOCAL_HEADS, GROUP * span_rows, 2 * HEAD_DIM)
    keys = 2 * len(held) * span_rows
    heads = LOCAL_HEADS // 2 if is_last else LOCAL_HEADS
    scratch = [pltpu.VMEM((keys, heads * HEAD_DIM), jnp.bfloat16)] * 2
    aliases = {}
    if not is_first:
        operands.append(before)
        specs.append(vmem)
    if is_last:
        operands += [array for _, array in everything]
        specs += [hbm] * len(everything)
        out_shape, out_specs = [], []
        if 0 in sides and not continued:
            out_shape.append(jax.ShapeDtypeStruct((2 * span_rows, 2 * width), jnp.bfloat16))
            out_specs.append(hbm)
        if 1 in sides or continued:
            out_shape.append(pltpu.VMEM((2 * span_rows, width // 2), jnp.bfloat16))
            out_specs.append(vmem)
        all_keys = 2 * sum(array.shape[0] for _, array in everything if array.shape[0] == 2) // 2 * span_rows
        all_keys += 2 * sum(array.shape[0] == 1 for _, array in everything) * span_rows
        if not continued:
            scratch = scratch + [pltpu.VMEM((2 * span_rows, width // 2), jnp.bfloat16)]
        scratch = scratch + [
            pltpu.VMEM((8, HEAD_DIM), jnp.float32),
            pltpu.VMEM((all_keys, HEAD_DIM), jnp.bfloat16),
            pltpu.VMEM((all_keys, HEAD_DIM), jnp.bfloat16),
            pltpu.SemaphoreType.DMA((COPY_PIECES,)),
            pltpu.SemaphoreType.DMA,
        ]
    elif is_first:
        out_shape = [pltpu.VMEM(sums, jnp.float32), pltpu.VMEM((4 * span_rows, width), jnp.bfloat16)]
        out_specs = [vmem, vmem]
        scratch = scratch + [pltpu.SemaphoreType.DMA((4,))]
    else:
        out_shape, out_specs = pltpu.VMEM(sums, jnp.float32), vmem
        aliases = {len(operands) - 1: 0}
    return pl.pallas_call(
        functools.partial(
            stage, [pack for pack, _ in held], [pack for pack, _ in everything], part, sides, continued
        ),
        out_shape=out_shape,
        in_specs=specs,
        out_specs=out_specs,
        scratch_shapes=scratch,
        input_output_aliases=aliases,
        compiler_params=pltpu.CompilerParams(vmem_limit_bytes=12 << 20),
        cost_estimate=pl.CostEstimate(flops=1, bytes_accessed=1, transcendentals=0),
        name="stage",
    )(*operands)


def shards(queries, keys_values, fold, doc_length):
    size = lax.axis_size("ctx")

    def swap(name, block, mask=1):
        with jax.named_scope("swap_" + name):
            return lax.ppermute(block, "ctx", [(i, i ^ mask) for i in range(size)])

    def send(name, block, even, odd):
        with jax.named_scope("send_" + name):
            return lax.ppermute(block, "ctx", [(i, i ^ (odd if i % 2 else even)) for i in range(size)])

    query_other = swap("q", queries)
    mine, other = run_prepare(keys_values)
    (fold, doc_length), other = lax.optimization_barrier(((fold, doc_length), other))
    other = swap("kv", other)
    table, other = lax.optimization_barrier((run_fill_table(fold, doc_length), other))
    near, far, across = (2, 4), (4, 2), (6, 6)
    held = [(Pack((0, 0), 0), mine), (Pack((0, 0), 1), other)]
    first = pltpu.with_memory_space_constraint(queries, pltpu.HBM)
    sums, query_block = run_stage(table, (first, query_other), None, held, part="first")

    def after(items, sums):
        arrays, sums = lax.optimization_barrier(([array for _, array in items], sums))
        return [(pack, array) for (pack, _), array in zip(items, arrays)], sums

    def more(items, sums):
        return run_stage(table, (query_block,), sums, items)

    if size == 8:
        a1, b1 = send("a1", mine, 2, 4), send("b1", other, 2, 4)
        (mine, other), sums = lax.optimization_barrier(((mine, other), sums))
        a2, b2 = send("a2", mine, 4, 2), send("b2", other, 4, 2)
        (a1, b1), sums = lax.optimization_barrier(((a1, b1), sums))
        e = send("e", a1, 4, 2)
        f0, f1 = send("f0", b1[:1], 4, 2), send("f1", b1[1:], 4, 2)
        firsts = [(Pack(near, 0), a1), (Pack(near, 1), b1)]
        sums = more(firsts, sums)
        seconds, sums = after([(Pack(far, 0), a2), (Pack(far, 1), b2)], sums)
        sums = more(seconds, sums)
        thirds, sums = after([(Pack(across, 0), e)], sums)
        sums = more(thirds, sums)
        f0, sums = lax.optimization_barrier((f0, sums))
        everything = held + firsts + seconds + thirds
        halves = [f0, f1]
    else:
        got = {0: (mine, other)}
        everything = list(held)
        for offset in range(2, size, 2):
            step = offset & -offset
            got[offset] = [swap("far", block, step) for block in got[offset ^ step]]
            items = [(Pack((offset, offset), n), block) for n, block in enumerate(got[offset])]
            if offset < size - 2:
                sums = more(items, sums)
                everything += items
            else:
                sums = more(items[:1], sums)
                everything += items[:1]
                halves = [items[1][1][:1], items[1][1][1:]]
        across = (size - 2, size - 2)
    last = [(Pack(across, 1), halves[0])]
    attended, rest0 = run_stage(table, (query_block,), sums, last, everything + last, 0, (0, 1))
    rest0 = swap("out0", rest0)
    halves[1], attended = lax.optimization_barrier((halves[1], attended))
    last = [(Pack(across, 1), halves[1])]
    rest1 = run_stage(table, (query_block,), sums, last, everything + last, 1, (1,))[0]
    rest1 = swap("out1", rest1)
    (rest0, block), sums = lax.optimization_barrier(((rest0, halves[1]), sums))
    last = [(Pack(across, 1), block)]
    own = run_stage(table, (query_block,), sums, last, everything + last, 1, (0,), True)[0]
    return run_place_rest(own, rest0, rest1, attended)


def solution(mesh):
    in_specs = (P(("dp", "ctx"), None), P(("dp", "ctx"), None, None), P("dp"), P("dp"))
    out_specs = P(("dp", "ctx"), None)
    return jax.shard_map(shards, mesh=mesh, in_specs=in_specs, out_specs=out_specs, check_vma=False)
```

```python
import functools
import math

import jax
import jax.numpy as jnp
from jax import lax
from jax.experimental import pallas as pl
from jax.experimental.pallas import tpu as pltpu
from jax.sharding import PartitionSpec as P

HEADS = 32
KV_HEADS = 8
HEAD_DIM = 128
GROUP = HEADS // KV_HEADS
LOCAL_HEADS = KV_HEADS // 2
SCALE = math.log2(math.e) / math.sqrt(HEAD_DIM)
LIMIT = 2.0**90
COPY_PIECES = 8
NT = (((1,), (1,)), ((), ()))


class Pack:
    def __init__(self, offset, other):
        self.offset, self.other = offset, other

    def places(self, fold):
        me = lax.axis_index("ctx")
        odd = me % 2
        device = me ^ (self.offset[0] + odd * (self.offset[1] - self.offset[0]) + self.other)
        return [fold[2 * device], fold[2 * device + 1]]


def prepare(kv_hbm, mine_ref, other_ref, kv_ref, sems):
    core = lax.axis_index("ctx") % 2
    half = kv_ref.shape[0] // 2
    rows = kv_ref.shape[0] // COPY_PIECES
    width = mine_ref.shape[4]
    copies = []
    for n in range(COPY_PIECES):
        at = slice(n * rows, (n + 1) * rows)
        copies.append(pltpu.make_async_copy(kv_hbm.at[at], kv_ref.at[at], sems.at[n]))
        copies[-1].start()
    for n in range(COPY_PIECES):
        copies[n].wait()
        j, to = n * rows // half, n * rows % half
        for out_ref, which in ((other_ref, 1 - core), (mine_ref, core)):
            for part in range(2):
                columns = pl.ds(pl.multiple_of((2 * which + part) * width, width), width)
                out_ref[part, j, :, to : to + rows] = jnp.swapaxes(kv_ref[n * rows : (n + 1) * rows, :, columns], 0, 1)


def run_prepare(keys_values):
    rows, two, width = keys_values.shape
    vmem = pl.BlockSpec(memory_space=pltpu.VMEM)
    return pl.pallas_call(
        prepare,
        out_shape=[pltpu.VMEM((2, 2, two, rows // 2, width // 4), jnp.bfloat16)] * 2,
        in_specs=[pl.BlockSpec(memory_space=pl.ANY)],
        out_specs=[vmem, vmem],
        scratch_shapes=[pltpu.VMEM((rows, two, width), jnp.bfloat16), pltpu.SemaphoreType.DMA((COPY_PIECES,))],
        cost_estimate=pl.CostEstimate(flops=1, bytes_accessed=1, transcendentals=0),
        name="prepare",
    )(pltpu.with_memory_space_constraint(keys_values, pltpu.HBM))


def fill_table(fold, length, table):
    for n in range(fold.shape[0]):
        table[n] = fold[n]
    table[fold.shape[0]] = length[0]


def run_fill_table(fold, doc_length):
    smem = pl.BlockSpec(memory_space=pltpu.SMEM)
    return pl.pallas_call(
        fill_table,
        out_shape=pltpu.SMEM((fold.shape[0] + 1,), jnp.int32),
        in_specs=[smem, smem],
        out_specs=smem,
        cost_estimate=pl.CostEstimate(flops=1, bytes_accessed=1, transcendentals=0),
        name="fill_table",
    )(fold, doc_length)


def part_columns(core, part, width):
    return pl.ds(pl.multiple_of((2 * core + part) * width, width), width)


def place_rest(own, block0, block1, attended, out_hbm, sems):
    core = lax.axis_index("ctx") % 2
    pieces = ((own, core, 1), (block1, 1 - core, 1), (block0, 1 - core, 0))
    copies = [
        pltpu.make_async_copy(piece, out_hbm.at[:, part_columns(which, part, piece.shape[1])], sems.at[n])
        for n, (piece, which, part) in enumerate(pieces)
    ]
    for copy in copies:
        copy.start()
    for copy in copies:
        copy.wait()


def run_place_rest(own, block0, block1, attended):
    vmem = pl.BlockSpec(memory_space=pltpu.VMEM)
    hbm = pl.BlockSpec(memory_space=pl.ANY)
    return pl.pallas_call(
        place_rest,
        out_shape=jax.ShapeDtypeStruct(attended.shape, attended.dtype),
        in_specs=[vmem, vmem, vmem, hbm],
        out_specs=hbm,
        scratch_shapes=[pltpu.SemaphoreType.DMA((3,))],
        input_output_aliases={3: 0},
        compiler_params=pltpu.CompilerParams(vmem_limit_bytes=4 << 20),
        name="place_rest",
    )(*[pltpu.with_memory_space_constraint(part, pltpu.VMEM) for part in (own, block0, block1)], attended)


def stage(held, every_pack, part, sides, continued, *refs):
    refs = list(refs)
    is_first, is_last = part == "first", bool(sides)
    fold = refs[0]
    if is_first:
        q_hbm, q_swapped, *rest = refs[1:]
    else:
        q_ref, *rest = refs[1:]
    packs, rest = rest[: len(held)], rest[len(held) :]
    if not is_first:
        before, rest = rest[0], rest[1:]
    if is_last:
        every, rest = rest[: len(every_pack)], rest[len(every_pack) :]
        if 0 in sides and not continued:
            out_hbm, rest = rest[0], rest[1:]
        if 1 in sides:
            rest_ref, rest = rest[0], rest[1:]
        if continued:
            out_ref, *rest = rest
            key_buf, value_buf, worst, keys_all, values_all, out_sems, sem = rest
        else:
            key_buf, value_buf, out_ref, worst, keys_all, values_all, out_sems, sem = rest
        worst[...] = jnp.ones_like(worst)
        heads = range(part * LOCAL_HEADS // 2, (part + 1) * LOCAL_HEADS // 2)
    else:
        heads = range(LOCAL_HEADS)
        if is_first:
            total, q_ref, key_buf, value_buf, q_sems = rest
        else:
            total, key_buf, value_buf = rest
    span_rows = q_ref.shape[0] // 4
    group_rows = GROUP * span_rows
    spans = fold.shape[0]
    me = lax.axis_index("ctx")
    core = me % 2
    length = fold[fold.shape[0] - 1]

    if is_first:
        half, width = q_swapped.shape[0] // 2, q_ref.shape[1]
        columns = pl.ds(pl.multiple_of(core * width, width), width)
        copies = [
            pltpu.make_async_copy(
                source.at[j * half : (j + 1) * half, columns],
                q_ref.at[(2 * n + j) * half : (2 * n + j + 1) * half],
                q_sems.at[2 * n + j],
            )
            for n, source in enumerate((q_hbm, q_swapped))
            for j in range(2)
        ]
        for copy in copies:
            copy.start()

    places = [place for pack in held for place in pack.places(fold)]
    for n, place in enumerate(places):
        rank = sum((other < place).astype(jnp.int32) for other in places)
        at = pl.ds(pl.multiple_of(rank * span_rows, span_rows), span_rows)
        source = packs[n // 2]
        width = source.shape[4]
        wanted = range(source.shape[0]) if not is_last or source.shape[0] == 1 else [part]
        for to, piece in enumerate(wanted):
            key_buf[at, to * width : (to + 1) * width] = source[piece, n % 2, 0]
            value_buf[at, to * width : (to + 1) * width] = source[piece, n % 2, 1]

    def query_place(i):
        return fold[2 * (me ^ (i // 2)) + i % 2]

    def column(head):
        return pl.ds(pl.multiple_of(head * HEAD_DIM, HEAD_DIM), HEAD_DIM)

    def rows_of(i):
        return pl.ds(pl.multiple_of(i * span_rows, span_rows), span_rows)

    def row_in_span():
        return lax.broadcasted_iota(jnp.int32, (group_rows, 1), 0) % span_rows

    def target_of(side):
        return rest_ref if side else out_ref

    def finish(side, i, g, real, sums):
        weight_sum = sums[:, HEAD_DIM:]
        guess = pl.reciprocal(weight_sum, approx=True)
        inverse = guess * (2.0 - weight_sum * guess)
        largest = jnp.maximum(weight_sum, guess).reshape(-1, 8, HEAD_DIM)
        worst[...] = jnp.maximum(worst[...], jnp.where(real, jnp.max(largest, axis=0), 1.0))
        value = (sums[:, :HEAD_DIM] * inverse).astype(jnp.bfloat16)
        for n in range(GROUP):
            target_of(side)[rows_of(i - 2 * side), column((g - heads[0]) * GROUP + n)] = value[
                n * span_rows : (n + 1) * span_rows
            ]

    def product_of(i, g, seen, change):
        query = jnp.concatenate([q_ref[rows_of(i), column(g * GROUP + n)] for n in range(GROUP)], axis=0)
        keys = key_buf[: seen * span_rows, column(g - heads[0])]
        scores = lax.dot_general(query, keys, NT, preferred_element_type=jnp.float32)
        weights = jnp.exp2(scores * SCALE)
        parts = [change(n, weights[:, n * span_rows : (n + 1) * span_rows]) for n in range(seen)]
        weights = jnp.concatenate(parts, axis=1) if seen > 1 else parts[0]
        ones = jnp.ones((seen * span_rows, HEAD_DIM), jnp.bfloat16)
        values = jnp.concatenate([value_buf[: seen * span_rows, column(g - heads[0])], ones], axis=1)
        return jnp.dot(weights.astype(jnp.bfloat16), values, preferred_element_type=jnp.float32)

    def visible_product(i, g):
        place = query_place(i)
        seen = sum((other <= place).astype(jnp.int32) for other in places)

        def change(n, weights):
            if not is_first:
                return jnp.where(seen > n, weights, 0.0)
            col = lax.broadcasted_iota(jnp.int32, (group_rows, span_rows), 1)
            slack = jnp.minimum(row_in_span(), length - 1 - place * span_rows) - col
            least = jnp.where(n == seen - 1, 0, jnp.where(n < seen, -2 * span_rows * spans, 2 * span_rows * spans))
            return jnp.where(slack >= least, weights, 0.0)

        return product_of(i, g, len(places), change)

    def add(i):
        for g in heads:
            total[i, g] = visible_product(i, g) if is_first else total[i, g] + visible_product(i, g)

    def add_last(side):
        for i in (2 * side, 2 * side + 1):
            for g in heads:
                finish(side, i, g, query_place(i) * span_rows < length, before[i, g] + visible_product(i, g))
        ends = [query_place(i) * span_rows + span_rows for i in (2 * side, 2 * side + 1)]

        @pl.when(jnp.maximum(ends[0], ends[1]) > length)
        def _():
            target = target_of(side)
            for i, end in enumerate(ends):
                row = end - span_rows + lax.broadcasted_iota(jnp.int32, (span_rows, target.shape[1]), 0)
                kept = jnp.where(row < length, target[rows_of(i), :].astype(jnp.float32), 0.0)
                target[rows_of(i), :] = kept.astype(jnp.bfloat16)

        if side == 0 and not continued:
            for i in range(2):
                out_copy(i).start()

    def out_copy(i):
        width = out_ref.shape[1]
        columns = part_columns(core, part, width)
        return pltpu.make_async_copy(out_ref.at[rows_of(i)], out_hbm.at[rows_of(i), columns], out_sems.at[i])

    if not is_last:
        for i in range(4):
            if is_first:
                copies[i].wait()
            add(i)
        return
    for side in sides:
        add_last(side)
    if 0 in sides and not continued:
        for i in range(2):
            out_copy(i).wait()

    @pl.when(jnp.logical_not(jnp.max(worst[...]) < LIMIT))
    def _():
        block = 4 * span_rows

        def again(side, step, piece, inside):
            i, n = step // GROUP + 2 * side, step % GROUP
            local = piece * (LOCAL_HEADS // 2) + inside if len(heads) == LOCAL_HEADS else inside
            place = query_place(i)
            query = q_ref[rows_of(i), column((heads[0] + local) * GROUP + n)]
            row = place * span_rows + lax.broadcasted_iota(jnp.int32, (span_rows, 1), 0)

            def masked(k):
                at = pl.ds(pl.multiple_of(k * block, block), block)
                raw = SCALE * lax.dot_general(query, keys_all[at, :], NT, preferred_element_type=jnp.float32)
                key_pos = k * block + lax.broadcasted_iota(jnp.int32, (span_rows, block), 1)
                return raw, key_pos <= jnp.minimum(row, length - 1), at

            def top(k, peak):
                raw, mask, _ = masked(k)
                return jnp.maximum(peak, jnp.max(jnp.where(mask, raw, -1e30), axis=1, keepdims=True))

            blocks = place // 4 + 1
            peak = lax.fori_loop(0, blocks, top, jnp.full((span_rows, 1), -1e30, jnp.float32))

            def more(k, sums):
                raw, mask, at = masked(k)
                weights = jnp.where(mask, jnp.exp2(raw - peak), 0.0)
                product = jnp.dot(weights.astype(jnp.bfloat16), values_all[at, :], preferred_element_type=jnp.float32)
                return sums[0] + product, sums[1] + jnp.sum(weights, axis=1, keepdims=True)

            zero = (jnp.zeros((span_rows, HEAD_DIM), jnp.float32), jnp.zeros((span_rows, 1), jnp.float32))
            numerator, weight_sum = lax.fori_loop(0, blocks, more, zero)
            value = jnp.where(row < length, numerator / weight_sum, 0.0)
            target_of(side)[rows_of(i - 2 * side), column(local * GROUP + n)] = value.astype(jnp.bfloat16)

        def one_head(inside, carry):
            for pack, source in zip(every_pack, every):
                piece = part if source.shape[0] == 2 else 0
                for j, place in enumerate(pack.places(fold)):
                    for kind, target in enumerate((keys_all, values_all)):
                        copy = pltpu.make_async_copy(
                            source.at[piece, j, kind, :, column(inside)], target.at[rows_of(place), :], sem
                        )
                        copy.start()
                        copy.wait()
            for side in sides:

                def one(step, carry):
                    again(side, step, 0, inside)
                    return carry

                lax.fori_loop(0, 2 * GROUP, one, 0)
            return carry

        lax.fori_loop(0, len(heads), one_head, 0)
        if 0 in sides and not continued:
            for i in range(2):
                out_copy(i).start()
                out_copy(i).wait()


def run_stage(table, query_blocks, before, held, everything=(), part=None, sides=(), continued=False):
    is_first, is_last = part == "first", bool(sides)
    span_rows = held[0][1].shape[3]
    width = HEADS // 2 * HEAD_DIM
    vmem = pl.BlockSpec(memory_space=pltpu.VMEM)
    smem = pl.BlockSpec(memory_space=pltpu.SMEM)
    hbm = pl.BlockSpec(memory_space=pl.ANY)
    operands = [table, *query_blocks, *[array for _, array in held]]
    specs = [smem] + [hbm if is_first else vmem] * len(query_blocks) + [vmem] * len(held)
    sums = (4, LOCAL_HEADS, GROUP * span_rows, 2 * HEAD_DIM)
    keys = 2 * len(held) * span_rows
    heads = LOCAL_HEADS // 2 if is_last else LOCAL_HEADS
    scratch = [pltpu.VMEM((keys, heads * HEAD_DIM), jnp.bfloat16)] * 2
    aliases = {}
    if not is_first:
        operands.append(before)
        specs.append(vmem)
    if is_last:
        operands += [array for _, array in everything]
        specs += [hbm] * len(everything)
        out_shape, out_specs = [], []
        if 0 in sides and not continued:
            out_shape.append(jax.ShapeDtypeStruct((2 * span_rows, 2 * width), jnp.bfloat16))
            out_specs.append(hbm)
        if 1 in sides or continued:
            out_shape.append(pltpu.VMEM((2 * span_rows, width // 2), jnp.bfloat16))
            out_specs.append(vmem)
        all_keys = 2 * sum(array.shape[0] for _, array in everything if array.shape[0] == 2) // 2 * span_rows
        all_keys += 2 * sum(array.shape[0] == 1 for _, array in everything) * span_rows
        if not continued:
            scratch = scratch + [pltpu.VMEM((2 * span_rows, width // 2), jnp.bfloat16)]
        scratch = scratch + [
            pltpu.VMEM((8, HEAD_DIM), jnp.float32),
            pltpu.VMEM((all_keys, HEAD_DIM), jnp.bfloat16),
            pltpu.VMEM((all_keys, HEAD_DIM), jnp.bfloat16),
            pltpu.SemaphoreType.DMA((COPY_PIECES,)),
            pltpu.SemaphoreType.DMA,
        ]
    elif is_first:
        out_shape = [pltpu.VMEM(sums, jnp.float32), pltpu.VMEM((4 * span_rows, width), jnp.bfloat16)]
        out_specs = [vmem, vmem]
        scratch = scratch + [pltpu.SemaphoreType.DMA((4,))]
    else:
        out_shape, out_specs = pltpu.VMEM(sums, jnp.float32), vmem
        aliases = {len(operands) - 1: 0}
    return pl.pallas_call(
        functools.partial(
            stage, [pack for pack, _ in held], [pack for pack, _ in everything], part, sides, continued
        ),
        out_shape=out_shape,
        in_specs=specs,
        out_specs=out_specs,
        scratch_shapes=scratch,
        input_output_aliases=aliases,
        compiler_params=pltpu.CompilerParams(vmem_limit_bytes=12 << 20),
        cost_estimate=pl.CostEstimate(flops=1, bytes_accessed=1, transcendentals=0),
        name="stage",
    )(*operands)


def shards(queries, keys_values, fold, doc_length):
    size = lax.axis_size("ctx")

    def swap(name, block, mask=1):
        with jax.named_scope("swap_" + name):
            return lax.ppermute(block, "ctx", [(i, i ^ mask) for i in range(size)])

    def send(name, block, even, odd):
        with jax.named_scope("send_" + name):
            return lax.ppermute(block, "ctx", [(i, i ^ (odd if i % 2 else even)) for i in range(size)])

    query_other = swap("q", queries)
    mine, other = run_prepare(keys_values)
    (fold, doc_length), other = lax.optimization_barrier(((fold, doc_length), other))
    other = swap("kv", other)
    table, other = lax.optimization_barrier((run_fill_table(fold, doc_length), other))
    near, far, across = (2, 4), (4, 2), (6, 6)
    held = [(Pack((0, 0), 0), mine), (Pack((0, 0), 1), other)]
    first = pltpu.with_memory_space_constraint(queries, pltpu.HBM)
    sums, query_block = run_stage(table, (first, query_other), None, held, part="first")

    def after(items, sums):
        arrays, sums = lax.optimization_barrier(([array for _, array in items], sums))
        return [(pack, array) for (pack, _), array in zip(items, arrays)], sums

    def more(items, sums):
        return run_stage(table, (query_block,), sums, items)

    if size == 8:
        a1, b1 = send("a1", mine, 2, 4), send("b1", other, 2, 4)
        (mine, other), sums = lax.optimization_barrier(((mine, other), sums))
        a2, b2 = send("a2", mine, 4, 2), send("b2", other, 4, 2)
        (a1, b1), sums = lax.optimization_barrier(((a1, b1), sums))
        e = send("e", a1, 4, 2)
        f0, f1 = send("f0", b1[:1], 4, 2), send("f1", b1[1:], 4, 2)
        firsts = [(Pack(near, 0), a1), (Pack(near, 1), b1)]
        sums = more(firsts, sums)
        seconds, sums = after([(Pack(far, 0), a2), (Pack(far, 1), b2)], sums)
        sums = more(seconds, sums)
        thirds, sums = after([(Pack(across, 0), e)], sums)
        sums = more(thirds, sums)
        f0, sums = lax.optimization_barrier((f0, sums))
        everything = held + firsts + seconds + thirds
        halves = [f0, f1]
    else:
        got = {0: (mine, other)}
        everything = list(held)
        for offset in range(2, size, 2):
            step = offset & -offset
            got[offset] = [swap("far", block, step) for block in got[offset ^ step]]
            items = [(Pack((offset, offset), n), block) for n, block in enumerate(got[offset])]
            if offset < size - 2:
                sums = more(items, sums)
                everything += items
            else:
                sums = more(items[:1], sums)
                everything += items[:1]
                halves = [items[1][1][:1], items[1][1][1:]]
        across = (size - 2, size - 2)
    last = [(Pack(across, 1), halves[0])]
    attended, rest0 = run_stage(table, (query_block,), sums, last, everything + last, 0, (0, 1))
    rest0 = swap("out0", rest0)
    halves[1], attended = lax.optimization_barrier((halves[1], attended))
    last = [(Pack(across, 1), halves[1])]
    rest1 = run_stage(table, (query_block,), sums, last, everything + last, 1, (1,))[0]
    rest1 = swap("out1", rest1)
    (rest0, block), sums = lax.optimization_barrier(((rest0, halves[1]), sums))
    last = [(Pack(across, 1), block)]
    own = run_stage(table, (query_block,), sums, last, everything + last, 1, (0,), True)[0]
    return run_place_rest(own, rest0, rest1, attended)


def solution(mesh):
    in_specs = (P(("dp", "ctx"), None), P(("dp", "ctx"), None, None), P("dp"), P("dp"))
    out_specs = P(("dp", "ctx"), None)
    return jax.shard_map(shards, mesh=mesh, in_specs=in_specs, out_specs=out_specs, check_vma=False)
```
